32 devices in a mesh: grp: 2 (over core), shard: 16 (over z, y, x).
Axes of the slice: x: 2, y: 2, z: 4, core: 2. Of those that a mesh axis runs over, the one named last changes fastest.
Arguments:
- embeddings: bfloat16 [32768, 768], P(('grp', 'shard')), may hold values from -0.26 to 0.26
- centers: bfloat16 [2048, 768], P('shard'), may hold values from -0.26 to 0.26
- assignment: int32 [32768, 1], P(('grp', 'shard')), may hold values from 0 to 2047, as said below
Outputs:
- old_min: float32 [32768], P(('grp', 'shard'))
- refined_centers: float32 [2048, 768], P('shard')
- new_min: float32 [32768], P(('grp', 'shard'))
The draws below stay inside these ranges and needn't reach their ends.
Inputs may be any that keep to these rules, and one draw needn't show every extreme that they name: `assignment`: every cluster is named by at least one row; cluster k belongs to the index of shard that holds centers[k]; the rows of one device name clusters belonging to any one index of shard at least 32 and at most 128 times, and in every group one index of shard is named 128 times by the rows of each device of that group.
All inputs are finite; a program needn't handle non-finite values.
Results may differ from the reference program's by a relative error of at most 0.0003.
Values may be sent and summed in bfloat16 or wider, within the bound.
A program may use at most 64 MiB of HBM per device.

```python
import math
import jax
import jax.numpy as jnp
from jax import lax

D = 768
K = 2048
ROW_DEV = 1024
ROWS = 32768
N_GRP = 2
N_SHARD = 16


def owner_layout(key):
    key = jax.random.fold_in(key, 101)
    keys = jax.random.split(key, 6)
    devices_all = N_GRP * N_SHARD
    most = 2 * ROW_DEV // N_SHARD
    fewest = ROW_DEV // (2 * N_SHARD)
    extra = ROW_DEV - most - (N_SHARD - 1) * fewest
    owned = K // N_SHARD
    group_full = jax.random.randint(keys[0], (N_GRP,), 0, N_SHARD).astype(jnp.int32)
    full = jnp.repeat(group_full, N_SHARD)
    others = jnp.arange(N_SHARD - 1, dtype=jnp.int32)[None, :]
    others = others + (others >= full[:, None]).astype(jnp.int32)
    fewest_part = jnp.repeat(others, fewest, axis=1)
    spare_pool = jnp.repeat(others, most - fewest, axis=1)
    pool_keys = jax.random.split(keys[1], devices_all)
    shuffled = jax.vmap(jax.random.permutation)(pool_keys, spare_pool)
    full_part = jnp.broadcast_to(full[:, None], (devices_all, most))
    tickets = jnp.concatenate([full_part, fewest_part, shuffled[:, :extra]], axis=1)
    row_keys = jax.random.split(keys[2], devices_all)
    owner = jax.vmap(jax.random.permutation)(row_keys, tickets).reshape(-1).astype(jnp.int32)
    owner_hot = (owner[:, None] == jnp.arange(N_SHARD, dtype=jnp.int32)[None, :]).astype(jnp.int32)
    ranked = jnp.sum(jnp.cumsum(owner_hot, axis=0) * owner_hot, axis=1) - 1
    rotate = jax.random.randint(keys[3], (N_SHARD,), 0, owned).astype(jnp.int32)
    loose = jnp.minimum(jax.random.randint(keys[4], (ROWS,), 0, owned), jax.random.randint(keys[5], (ROWS,), 0, owned)).astype(jnp.int32)
    within = jnp.where(ranked < owned, ranked, loose)
    within = (within + rotate[owner]) % owned
    return (owner * owned + within).astype(jnp.int32)


def cluster_bases(key):
    key = jax.random.fold_in(key, 202)
    keys = jax.random.split(key, 4)
    gauss = jnp.clip(jax.random.normal(keys[0], (K, D), jnp.float32), -3.5, 3.5)
    order = jax.random.permutation(keys[3], K).astype(jnp.int32)
    return (gauss, order)


def draw_assignment(key, part):
    labels = owner_layout(key)
    return labels[:, None]


def draw_embeddings(key, part):
    labels = owner_layout(key)
    gauss, order = cluster_bases(key)
    key = jax.random.fold_in(key, 5)
    keys = jax.random.split(key, 4)
    stale = jax.random.randint(keys[2], (ROWS,), 0, 100) < 35
    elsewhere = jax.random.randint(keys[3], (ROWS,), 0, K).astype(jnp.int32)
    source = jnp.where(stale, elsewhere, labels).astype(jnp.int32)
    middle = 0.03 * gauss
    spread = jnp.exp(jax.random.uniform(keys[0], (ROWS, 1), jnp.float32, math.log(0.012), math.log(0.036)))
    noise = jnp.clip(jax.random.normal(keys[1], (ROWS, D), jnp.float32), -4.0, 4.0)
    return (middle[source] + spread * noise).astype(jnp.bfloat16)


def draw_centers(key, part):
    gauss, order = cluster_bases(key)
    key = jax.random.fold_in(key, 7)
    keys = jax.random.split(key, 2)
    middle = 0.03 * gauss
    spread = jnp.exp(jax.random.uniform(keys[0], (K, 1), jnp.float32, math.log(0.012), math.log(0.036)))
    noise = jnp.clip(jax.random.normal(keys[1], (K, D), jnp.float32), -4.0, 4.0)
    return (middle[order] + spread * noise).astype(jnp.bfloat16)


def setup_inputs(seed: int = 0) -> dict:
    key_list = jax.random.split(jax.random.key(seed), 4)
    embeddings = draw_embeddings(jax.random.fold_in(key_list[3], 71), 0)
    centers = draw_centers(jax.random.fold_in(key_list[3], 71), 0)
    assignment = draw_assignment(jax.random.fold_in(key_list[3], 71), 0)
    return {"embeddings": embeddings, "centers": centers, "assignment": assignment}


def nearest_old(embeddings, centers_b):
    center_norms = jnp.sum(jnp.square(centers_b.astype(jnp.float32)), 1)
    blocks = embeddings.reshape(-1, ROW_DEV, D)

    def one_block(block_rows):
        row_norms = jnp.sum(jnp.square(block_rows.astype(jnp.float32)), 1)
        products = jnp.dot(block_rows, centers_b.T, preferred_element_type=jnp.float32)
        distance = row_norms[:, None] - 2.0 * products + center_norms[None, :]
        return jnp.min(distance, 1)

    return lax.map(one_block, blocks).reshape(-1)


def nearest_new(embeddings, refined):
    center_norms = jnp.sum(jnp.square(refined), 1)
    blocks = embeddings.reshape(-1, ROW_DEV, D)

    def one_block(block_rows):
        wide_rows = block_rows.astype(jnp.float32)
        row_norms = jnp.sum(jnp.square(wide_rows), 1)
        products = jnp.dot(wide_rows, refined.T, precision=lax.Precision.HIGHEST, preferred_element_type=jnp.float32)
        distance = row_norms[:, None] - 2.0 * products + center_norms[None, :]
        return jnp.min(distance, 1)

    return lax.map(one_block, blocks).reshape(-1)


def reference(embeddings, centers, assignment):
    old_min = nearest_old(embeddings, centers)
    labels = assignment[:, 0].astype(jnp.int32)
    totals = jax.ops.segment_sum(embeddings.astype(jnp.float32), labels, num_segments=K)
    counts = jax.ops.segment_sum(jnp.ones((labels.shape[0],), jnp.float32), labels, num_segments=K)
    refined_centers = totals / counts[:, None]
    new_min = nearest_new(embeddings, refined_centers)
    return old_min, refined_centers, new_min
```

```python
import jax
import jax.numpy as jnp
from jax import lax
from jax.experimental import pallas as pl
from jax.experimental.pallas import tpu as pltpu
from jax.sharding import PartitionSpec as P

MESH = pl.DeviceIdType.MESH
CHIPS = {"grp": 2, "shard": 16}
SLICES = (2, 1, 3, 0)


def dot_nt(left, right):
    return lax.dot_general(
        left, right, (((1,), (1,)), ((), ())), preferred_element_type=jnp.float32
    )


def square_sums(values):
    wide = values.astype(jnp.float32)
    square = wide * wide
    high = square.astype(jnp.bfloat16)
    low = (square - high.astype(jnp.float32)).astype(jnp.bfloat16)
    ones = jnp.ones((16, values.shape[1]), jnp.bfloat16)
    return dot_nt(ones, high) + dot_nt(ones, low)


def kernel(
    emb, cen, lab, old_out, refined_out, new_out,
    tot, in1, in2, in3, rows, labels, old_all, new_all, scaled, norms,
    halves, mine, old_acc, new_acc, local_sem, send_sem, recv_sem,
):
    c = lax.axis_index("grp")
    s = lax.axis_index("shard")
    x, y, z = s % 2, (s // 2) % 2, s // 4
    owned, width = cen.shape
    half = width // 2
    n_rows = emb.shape[0]
    x1, y1 = x + (1 - c) * (1 - 2 * x), y + c * (1 - 2 * y)
    x2, y2 = x + c * (1 - 2 * x), y + (1 - c) * (1 - 2 * y)

    def at(zz, yy, xx):
        return zz * 4 + yy * 2 + xx

    sib = (1 - c, s)
    p1 = (c, at(z, y1, x1))
    p2 = (c, at(z, y2, x2))
    above = [None] + [(c, at((z + j) % 4, y, x)) for j in (1, 2, 3)]
    cols = pl.ds(pl.multiple_of(c * half, 128), half)
    other_cols = pl.ds(pl.multiple_of((1 - c) * half, 128), half)

    sent = []

    def send(src, dst, device):
        i = len(sent)
        copy = pltpu.make_async_remote_copy(
            src_ref=src, dst_ref=dst, send_sem=send_sem.at[i], recv_sem=recv_sem.at[i],
            device_id=device, device_id_type=MESH,
        )
        copy.start()
        sent.append(copy)
        return copy

    barrier = pltpu.get_barrier_semaphore()
    for peer in (sib, p1, p2, above[1], above[2], above[3]):
        pl.semaphore_signal(barrier, inc=1, device_id=peer, device_id_type=MESH)
    own_rows = pltpu.make_async_copy(emb.at[:, cols], rows.at[0], local_sem.at[0])
    own_rows.start()
    own_old = pltpu.make_async_copy(cen, old_all.at[s], local_sem.at[1])
    own_old.start()
    labels[0:8, :] = lab[...]
    old_acc[...] = jnp.full(old_acc.shape, jnp.inf, jnp.float32)
    new_acc[...] = jnp.full(new_acc.shape, jnp.inf, jnp.float32)
    pl.semaphore_wait(barrier, 6)

    rows_in = send(emb.at[:, other_cols], rows.at[1], sib)
    labels_in = send(lab, labels.at[pl.ds(8, 8)], sib)

    class Gather:
        def __init__(self, own, buf, share_own):
            self.buf = buf
            spot = buf.at[s, :, cols]
            self.z = [None] + [send(own, spot, above[j]) for j in (1, 2, 3)]
            self.d1 = [send(own, spot, p1)]
            self.d2 = [send(own, spot, p2)]
            self.fz = [send(own, spot, sib) if share_own else None]
            self.f1, self.f2, self.far, self.ffar = [], [], [], []

        def spot(self, j, yy, xx):
            return self.buf.at[at((z + 4 - j) % 4, yy, xx), :, cols]

        def along_z(self):
            for j in (1, 2, 3):
                self.z[j].wait_recv()
                spot = self.spot(j, y, x)
                self.d1.append(send(spot, spot, p1))
                self.d2.append(send(spot, spot, p2))
                self.fz.append(send(spot, spot, sib))

        def along_d1(self):
            for j in range(4):
                self.d1[j].wait_recv()
                spot = self.spot(j, y1, x1)
                self.far.append(send(spot, spot, p2))
                self.f1.append(send(spot, spot, sib))

        def along_d2(self):
            for j in range(4):
                self.d2[j].wait_recv()
                spot = self.spot(j, y2, x2)
                self.f2.append(send(spot, spot, sib))

        def last(self):
            for j in range(4):
                self.far[j].wait_recv()
                spot = self.spot(j, 1 - y, 1 - x)
                self.ffar.append(send(spot, spot, sib))

        def need(self, copies):
            for copy in copies:
                if copy is not None:
                    copy.wait_recv()

    def nearest(buf, acc, yy, xx):
        def pair(i, carry):
            first = at((z + 4 - 2 * i) % 4, yy, xx)
            second = at((z + 3 - 2 * i) % 4, yy, xx)
            block = jnp.concatenate([buf[first], buf[second]], 0)
            distance = dot_nt(scaled[...], block) + square_sums(block)[0:1, :]
            near = jnp.minimum(distance[:, :owned], distance[:, owned:])
            acc[...] = jnp.minimum(acc[...], near)
            return carry

        lax.fori_loop(0, 2, pair, 0)

    old = Gather(cen.at[:, cols], old_all, False)

    wide = emb[...]
    scaled[...] = wide * jnp.asarray(-2.0, jnp.bfloat16)
    norms[...] = square_sums(wide)[0:8, :]

    own_rows.wait()
    rows_in.wait_recv()
    labels_in.wait_recv()

    def totals(j):
        def one(f, carry):
            fa, fb = f // 2, f % 2
            xa = x + fa * (x1 - x) + fb * (x2 - x)
            ya = y + fa * (y1 - y) + fb * (y2 - y)
            base = at((z + j) % 4, ya, xa) * owned
            ids = lax.broadcasted_iota(jnp.int32, (owned, 128), 0) + base
            hot = [
                (labels[r : r + 1, :] == ids).astype(jnp.float32).astype(jnp.bfloat16)
                for r in range(16)
            ]
            part = jnp.zeros((owned, half), jnp.float32)
            count = jnp.zeros((16, owned), jnp.float32)
            ones = jnp.ones((16, n_rows), jnp.bfloat16)
            for g in range(2):
                block = jnp.concatenate(hot[8 * g : 8 * g + 8], 1)
                part += jnp.dot(block, rows[g], preferred_element_type=jnp.float32)
                count += dot_nt(ones, block)
            tot[4 * j + f, 0:owned, :] = part
            tot[4 * j + f, owned : owned + 8, :] = jnp.concatenate([count[0:8]] * (half // owned), 1)
            return carry

        lax.fori_loop(0, 4, one, 0)

    stage1, stage2, stage3 = {}, {}, {}
    for j in SLICES:
        totals(j)
        stage1[j] = send(tot.at[pl.ds(4 * j + 2, 2)], in1.at[j], p1)
    old.along_z()

    def settle(j):
        stage2[j].wait_recv()
        tot[4 * j] += in2[j]
        if j > 0:
            stage3[j] = send(tot.at[4 * j], in3.at[j - 1], above[j])

    for i, j in enumerate(SLICES):
        stage1[j].wait_recv()
        tot[4 * j] += in1[j, 0]
        tot[4 * j + 1] += in1[j, 1]
        stage2[j] = send(tot.at[4 * j + 1], in2.at[j], p2)
        if i > 0:
            settle(SLICES[i - 1])
    settle(SLICES[-1])
    old.along_d1()

    for j in (1, 2, 3):
        stage3[j].wait_recv()
    total = tot[0] + in3[0] + in3[1] + in3[2]
    count = jnp.broadcast_to(total[owned : owned + 1, 0:owned], (owned, owned)).T
    refined = total[0:owned, :] / jnp.concatenate([count] * (half // owned), 1)
    halves[c] = refined
    mine[...] = refined.astype(jnp.bfloat16)
    own_new = pltpu.make_async_copy(mine, new_all.at[s, :, cols], local_sem.at[2])
    own_new.start()
    new = Gather(mine, new_all, True)
    half_in = send(halves.at[c], halves.at[c], sib)

    old.along_d2()
    old.last()
    own_old.wait()
    old.need(old.fz)
    nearest(old_all, old_acc, y, x)
    new.along_z()
    old.need(old.f1)
    old.need(old.f2)
    nearest(old_all, old_acc, y1, x1)
    nearest(old_all, old_acc, y2, x2)
    new.along_d1()
    new.along_d2()
    old.need(old.ffar)
    nearest(old_all, old_acc, 1 - y, 1 - x)

    own_new.wait()
    new.need(new.fz)
    nearest(new_all, new_acc, y, x)
    new.last()
    new.need(new.f1)
    new.need(new.f2)
    nearest(new_all, new_acc, y1, x1)
    nearest(new_all, new_acc, y2, x2)
    half_in.wait_recv()
    refined_out[:, 0:half] = halves[0]
    refined_out[:, half:width] = halves[1]
    old_out[...] = jnp.min(old_acc[...].T, 0, keepdims=True) + norms[0:1, :]
    new.need(new.ffar)
    nearest(new_all, new_acc, 1 - y, 1 - x)
    new_out[...] = jnp.min(new_acc[...].T, 0, keepdims=True) + norms[0:1, :]
    for copy in sent:
        copy.wait_send()


COPIES = 80


def in_one_kernel(embeddings, centers, assignment):
    n_rows, width = embeddings.shape
    owned = centers.shape[0]
    half = width // 2
    f32, bf16 = jnp.float32, jnp.bfloat16
    vmem = pl.BlockSpec(memory_space=pltpu.VMEM)
    old_min, refined, new_min = pl.pallas_call(
        kernel,
        out_shape=(
            jax.ShapeDtypeStruct((1, n_rows), f32),
            jax.ShapeDtypeStruct((owned, width), f32),
            jax.ShapeDtypeStruct((1, n_rows), f32),
        ),
        in_specs=[vmem] * 3,
        out_specs=(vmem,) * 3,
        scratch_shapes=[
            pltpu.VMEM((16, owned + 8, half), f32),
            pltpu.VMEM((4, 2, owned + 8, half), f32),
            pltpu.VMEM((4, owned + 8, half), f32),
            pltpu.VMEM((3, owned + 8, half), f32),
            pltpu.VMEM((2, n_rows, half), bf16),
            pltpu.VMEM((16, 128), jnp.int32),
            pltpu.VMEM((16, owned, width), bf16),
            pltpu.VMEM((16, owned, width), bf16),
            pltpu.VMEM((n_rows, width), bf16),
            pltpu.VMEM((8, n_rows), f32),
            pltpu.VMEM((2, owned, half), f32),
            pltpu.VMEM((owned, half), bf16),
            pltpu.VMEM((n_rows, owned), f32),
            pltpu.VMEM((n_rows, owned), f32),
            pltpu.SemaphoreType.DMA((3,)),
            pltpu.SemaphoreType.DMA((COPIES,)),
            pltpu.SemaphoreType.DMA((COPIES,)),
        ],
        compiler_params=pltpu.CompilerParams(
            collective_id=0, has_side_effects=True, vmem_limit_bytes=48 * 1024 * 1024
        ),
        cost_estimate=pl.CostEstimate(
            flops=6 * n_rows * 16 * owned * width, bytes_accessed=8 * n_rows * width, transcendentals=0
        ),
        name="lloyd_step",
    )(embeddings, centers, assignment.reshape(n_rows // 128, 128))
    return old_min.reshape(n_rows), refined, new_min.reshape(n_rows)


def on_device(embeddings, centers, assignment):
    wide_rows = embeddings.astype(jnp.float32)
    row_norms = jnp.sum(jnp.square(wide_rows), 1)
    starting = jnp.full((embeddings.shape[0],), jnp.inf, jnp.float32)
    portion = lax.all_gather(centers, "shard", axis=0, tiled=True)
    portion_norms = jnp.sum(jnp.square(portion.astype(jnp.float32)), 1)
    products = lax.dot_general(
        embeddings, portion, (((1,), (1,)), ((), ())), preferred_element_type=jnp.float32
    )
    distance = row_norms[:, None] - 2.0 * products + portion_norms[None, :]
    old_min = jnp.minimum(starting, jnp.min(distance, 1))
    n_shard = lax.axis_size("shard")
    owned = centers.shape[0]
    clusters = owned * n_shard
    labels = assignment[:, 0]
    onehot = (labels[:, None] == jnp.arange(clusters, dtype=jnp.int32)[None, :]).astype(
        jnp.bfloat16
    )
    partial_totals = lax.dot_general(
        onehot, embeddings, (((0,), (0,)), ((), ())), preferred_element_type=jnp.float32
    )
    partial_counts = jnp.sum(onehot, 0, dtype=jnp.float32)
    owner_totals, owner_counts = (
        lax.psum_scatter(partial_totals, "shard", scatter_dimension=0, tiled=True),
        lax.psum_scatter(partial_counts, "shard", scatter_dimension=0, tiled=True),
    )
    totals, counts = lax.psum((owner_totals, owner_counts), "grp")
    refined_centers = totals / counts[:, None]
    portion = lax.all_gather(refined_centers, "shard", axis=0, tiled=True)
    portion_norms = jnp.sum(jnp.square(portion), 1)
    products = lax.dot_general(
        wide_rows,
        portion,
        (((1,), (1,)), ((), ())),
        precision=lax.Precision.HIGHEST,
        preferred_element_type=jnp.float32,
    )
    distance = row_norms[:, None] - 2.0 * products + portion_norms[None, :]
    new_min = jnp.minimum(starting, jnp.min(distance, 1))
    return (old_min, refined_centers, new_min)


def solution(mesh):
    placed = (P(("grp", "shard"), None), P("shard", None), P(("grp", "shard"), None))
    here = dict(mesh.shape) == CHIPS
    return jax.shard_map(
        in_one_kernel if here else on_device,
        mesh=mesh,
        in_specs=placed,
        out_specs=(P(("grp", "shard")), P("shard", None), P(("grp", "shard"))),
        check_vma=False,
    )
```

```python
import jax
import jax.numpy as jnp
from jax import lax
from jax.experimental import pallas as pl
from jax.experimental.pallas import tpu as pltpu
from jax.sharding import PartitionSpec as P

MESH = pl.DeviceIdType.MESH
CHIPS = {"grp": 2, "shard": 16}
SLICES = (2, 1, 3, 0)


def dot_nt(left, right):
    return lax.dot_general(
        left, right, (((1,), (1,)), ((), ())), preferred_element_type=jnp.float32
    )


def square_sums(values):
    wide = values.astype(jnp.float32)
    square = wide * wide
    high = square.astype(jnp.bfloat16)
    low = (square - high.astype(jnp.float32)).astype(jnp.bfloat16)
    ones = jnp.ones((16, values.shape[1]), jnp.bfloat16)
    return dot_nt(ones, high) + dot_nt(ones, low)


def column(row):
    return jnp.broadcast_to(row, (128, 128)).T


def pack(block, whole, meta):
    half = whole.shape[1]
    values, count = block[:, 0:half], block[:, half:]
    most = jnp.maximum(jnp.max(jnp.abs(values), 1, keepdims=True), 1e-30)
    whole[...] = jnp.round(values * (32767.0 / most)).astype(jnp.int32).astype(jnp.int16)
    scale = jnp.broadcast_to(most * (1.0 / 32767.0), count.shape)
    lane = lax.broadcasted_iota(jnp.int32, count.shape, 1)
    meta[...] = jnp.where(lane < 4, count, scale).T[0:8]


def unpack(whole, meta):
    half = whole.shape[1]
    count, scale = column(meta[0:1, :]), column(meta[4:5, :])
    values = whole[...].astype(jnp.int32).astype(jnp.float32)
    return jnp.concatenate([values * jnp.concatenate([scale] * (half // 128), 1), count], 1)


def kernel(
    emb, cen, lab, old_out, refined_out, new_out,
    tot, out1, meta1, in1, min1, out2, meta2, in2, min2, out3, meta3, in3, min3,
    rows, labels, old_all, new_all, here, scaled, norms,
    halves, mine, old_acc, new_acc, local_sem, send_sem, recv_sem,
):
    c = lax.axis_index("grp")
    s = lax.axis_index("shard")
    x, y, z = s % 2, (s // 2) % 2, s // 4
    owned, width = cen.shape
    half = width // 2
    n_rows = emb.shape[0]
    x1, y1 = x + (1 - c) * (1 - 2 * x), y + c * (1 - 2 * y)
    x2, y2 = x + c * (1 - 2 * x), y + (1 - c) * (1 - 2 * y)

    def at(zz, yy, xx):
        return zz * 4 + yy * 2 + xx

    sib = (1 - c, s)
    p1 = (c, at(z, y1, x1))
    p2 = (c, at(z, y2, x2))
    above = [None] + [(c, at((z + j) % 4, y, x)) for j in (1, 2, 3)]
    cols = pl.ds(pl.multiple_of(c * half, 128), half)
    other_cols = pl.ds(pl.multiple_of((1 - c) * half, 128), half)

    sent = []

    def send(src, dst, device):
        i = len(sent)
        copy = pltpu.make_async_remote_copy(
            src_ref=src, dst_ref=dst, send_sem=send_sem.at[i], recv_sem=recv_sem.at[i],
            device_id=device, device_id_type=MESH,
        )
        copy.start()
        sent.append(copy)
        return copy

    barrier = pltpu.get_barrier_semaphore()
    for peer in (sib, p1, p2, above[1], above[2], above[3]):
        pl.semaphore_signal(barrier, inc=1, device_id=peer, device_id_type=MESH)
    own_lab = pltpu.make_async_copy(lab, labels.at[pl.ds(0, 8)], local_sem.at[3])
    own_lab.start()
    own_emb = pltpu.make_async_copy(emb, here, local_sem.at[4])
    own_emb.start()
    own_rows = pltpu.make_async_copy(emb.at[:, cols], rows.at[0, :, pl.ds(0, half)], local_sem.at[0])
    own_rows.start()
    own_old = pltpu.make_async_copy(cen, old_all.at[s], local_sem.at[1])
    own_old.start()
    rows[:, :, half:] = jnp.ones((2, n_rows, 128), jnp.bfloat16)
    old_acc[...] = jnp.full(old_acc.shape, jnp.inf, jnp.float32)
    new_acc[...] = jnp.full(new_acc.shape, jnp.inf, jnp.float32)
    pl.semaphore_wait(barrier, 6)

    rows_in = send(emb.at[:, other_cols], rows.at[1, :, pl.ds(0, half)], sib)
    labels_in = send(lab, labels.at[pl.ds(8, 8)], sib)

    class Gather:
        def __init__(self, own, buf, share_own):
            self.buf = buf
            spot = buf.at[s, :, cols]
            self.z = [None] + [send(own, spot, above[j]) for j in (1, 2, 3)]
            self.d1 = [send(own, spot, p1)]
            self.d2 = [send(own, spot, p2)]
            self.fz = [send(own, spot, sib) if share_own else None]
            self.f1, self.f2, self.far, self.ffar = [], [], [], []

        def spot(self, j, yy, xx):
            return self.buf.at[at((z + 4 - j) % 4, yy, xx), :, cols]

        def along_z(self):
            for j in (1, 2, 3):
                self.z[j].wait_recv()
                spot = self.spot(j, y, x)
                self.d1.append(send(spot, spot, p1))
                self.d2.append(send(spot, spot, p2))
                self.fz.append(send(spot, spot, sib))

        def along_d1(self):
            for j in range(4):
                self.d1[j].wait_recv()
                spot = self.spot(j, y1, x1)
                self.far.append(send(spot, spot, p2))
                self.f1.append(send(spot, spot, sib))

        def along_d2(self):
            for j in range(4):
                self.d2[j].wait_recv()
                spot = self.spot(j, y2, x2)
                self.f2.append(send(spot, spot, sib))

        def last(self):
            for j in range(4):
                self.far[j].wait_recv()
                spot = self.spot(j, 1 - y, 1 - x)
                self.ffar.append(send(spot, spot, sib))

        def need(self, copies):
            for copy in copies:
                if copy is not None:
                    copy.wait_recv()

    def nearest(buf, acc, yy, xx):
        def pair(i, carry):
            first = at((z + 4 - 2 * i) % 4, yy, xx)
            second = at((z + 3 - 2 * i) % 4, yy, xx)
            block = jnp.concatenate([buf[first], buf[second]], 0)
            distance = dot_nt(scaled[...], block) + square_sums(block)[0:1, :]
            near = jnp.minimum(distance[:, :owned], distance[:, owned:])
            acc[...] = jnp.minimum(acc[...], near)
            return carry

        lax.fori_loop(0, 2, pair, 0)

    old = Gather(cen.at[:, cols], old_all, False)

    own_emb.wait()
    wide = here[...]
    scaled[...] = wide * jnp.asarray(-2.0, jnp.bfloat16)
    norms[...] = square_sums(wide)[0:8, :]

    own_lab.wait()
    own_rows.wait()
    rows_in.wait_recv()
    labels_in.wait_recv()

    def partial(j, fa, fb):
        xa = x + fa * (x1 - x) + fb * (x2 - x)
        ya = y + fa * (y1 - y) + fb * (y2 - y)
        base = at((z + j) % 4, ya, xa) * owned
        ids = lax.broadcasted_iota(jnp.int32, (owned, 128), 0) + base
        hot = [
            (labels[r : r + 1, :] == ids).astype(jnp.float32).astype(jnp.bfloat16)
            for r in range(16)
        ]
        part = jnp.zeros((owned, half + 128), jnp.float32)
        for g in range(2):
            block = jnp.concatenate(hot[8 * g : 8 * g + 8], 1)
            part += jnp.dot(block, rows[g], preferred_element_type=jnp.float32)
        return part

    stage1, stage2, stage3 = {}, {}, {}

    def begin(j):
        def away(fb, carry):
            pack(partial(j, 1, fb), out1.at[j, fb], meta1.at[j, fb])
            return carry

        def kept(fb, carry):
            tot[2 * j + fb] = partial(j, 0, fb)
            return carry

        lax.fori_loop(0, 2, away, 0)
        stage1[j] = (send(out1.at[j], in1.at[j], p1), send(meta1.at[j], min1.at[j], p1))
        lax.fori_loop(0, 2, kept, 0)

    def middle(j):
        for copy in stage1[j]:
            copy.wait_recv()
        pack(tot[2 * j + 1] + unpack(in1.at[j, 1], min1.at[j, 1]), out2.at[j], meta2.at[j])
        stage2[j] = (send(out2.at[j], in2.at[j], p2), send(meta2.at[j], min2.at[j], p2))
        tot[2 * j] += unpack(in1.at[j, 0], min1.at[j, 0])

    def settle(j):
        for copy in stage2[j]:
            copy.wait_recv()
        tot[2 * j] += unpack(in2.at[j], min2.at[j])
        if j > 0:
            i = j - 1
            pack(tot[2 * j], out3.at[i], meta3.at[i])
            stage3[j] = (send(out3.at[i], in3.at[i], above[j]), send(meta3.at[i], min3.at[i], above[j]))

    begin(SLICES[0])
    begin(SLICES[1])
    old.along_z()
    middle(SLICES[0])
    begin(SLICES[2])
    middle(SLICES[1])
    settle(SLICES[0])
    begin(SLICES[3])
    middle(SLICES[2])
    settle(SLICES[1])
    old.along_d1()
    middle(SLICES[3])
    settle(SLICES[2])
    settle(SLICES[3])
    old.along_d2()

    total = tot[0]
    for j in SLICES[:3]:
        for copy in stage3[j]:
            copy.wait_recv()
        total += unpack(in3.at[j - 1], min3.at[j - 1])
    refined = total[:, 0:half] / jnp.concatenate([total[:, half:]] * (half // 128), 1)
    halves[c] = refined
    mine[...] = refined.astype(jnp.bfloat16)
    own_new = pltpu.make_async_copy(mine, new_all.at[s, :, cols], local_sem.at[2])
    own_new.start()
    new = Gather(mine, new_all, True)
    half_in = send(halves.at[c], halves.at[c], sib)

    old.last()
    own_old.wait()
    old.need(old.fz)
    nearest(old_all, old_acc, y, x)
    new.along_z()
    old.need(old.f1)
    old.need(old.f2)
    nearest(old_all, old_acc, y1, x1)
    nearest(old_all, old_acc, y2, x2)
    new.along_d1()
    new.along_d2()
    old.need(old.ffar)
    nearest(old_all, old_acc, 1 - y, 1 - x)

    own_new.wait()
    new.need(new.fz)
    nearest(new_all, new_acc, y, x)
    new.last()
    new.need(new.f1)
    new.need(new.f2)
    nearest(new_all, new_acc, y1, x1)
    nearest(new_all, new_acc, y2, x2)
    half_in.wait_recv()
    refined_out[:, 0:half] = halves[0]
    refined_out[:, half:width] = halves[1]
    old_out[...] = jnp.min(old_acc[...].T, 0, keepdims=True) + norms[0:1, :]
    new.need(new.ffar)
    nearest(new_all, new_acc, 1 - y, 1 - x)
    new_out[...] = jnp.min(new_acc[...].T, 0, keepdims=True) + norms[0:1, :]
    for copy in sent:
        copy.wait_send()


COPIES = 96


def in_one_kernel(embeddings, centers, assignment):
    n_rows, width = embeddings.shape
    owned = centers.shape[0]
    half = width // 2
    f32, bf16, i16 = jnp.float32, jnp.bfloat16, jnp.int16
    vmem = pl.BlockSpec(memory_space=pltpu.VMEM)
    old_min, refined, new_min = pl.pallas_call(
        kernel,
        out_shape=(
            jax.ShapeDtypeStruct((1, n_rows), f32),
            jax.ShapeDtypeStruct((owned, width), f32),
            jax.ShapeDtypeStruct((1, n_rows), f32),
        ),
        in_specs=[pl.BlockSpec(memory_space=pl.ANY)] * 3,
        out_specs=(vmem,) * 3,
        scratch_shapes=[
            pltpu.VMEM((8, owned, half + 128), f32),
            pltpu.VMEM((4, 2, owned, half), i16),
            pltpu.VMEM((4, 2, 8, 128), f32),
            pltpu.VMEM((4, 2, owned, half), i16),
            pltpu.VMEM((4, 2, 8, 128), f32),
            pltpu.VMEM((4, owned, half), i16),
            pltpu.VMEM((4, 8, 128), f32),
            pltpu.VMEM((4, owned, half), i16),
            pltpu.VMEM((4, 8, 128), f32),
            pltpu.VMEM((3, owned, half), i16),
            pltpu.VMEM((3, 8, 128), f32),
            pltpu.VMEM((3, owned, half), i16),
            pltpu.VMEM((3, 8, 128), f32),
            pltpu.VMEM((2, n_rows, half + 128), bf16),
            pltpu.VMEM((16, 128), jnp.int32),
            pltpu.VMEM((16, owned, width), bf16),
            pltpu.VMEM((16, owned, width), bf16),
            pltpu.VMEM((n_rows, width), bf16),
            pltpu.VMEM((n_rows, width), bf16),
            pltpu.VMEM((8, n_rows), f32),
            pltpu.VMEM((2, owned, half), f32),
            pltpu.VMEM((owned, half), bf16),
            pltpu.VMEM((n_rows, owned), f32),
            pltpu.VMEM((n_rows, owned), f32),
            pltpu.SemaphoreType.DMA((5,)),
            pltpu.SemaphoreType.DMA((COPIES,)),
            pltpu.SemaphoreType.DMA((COPIES,)),
        ],
        compiler_params=pltpu.CompilerParams(
            collective_id=0, has_side_effects=True, vmem_limit_bytes=48 * 1024 * 1024
        ),
        cost_estimate=pl.CostEstimate(
            flops=6 * n_rows * 16 * owned * width, bytes_accessed=8 * n_rows * width, transcendentals=0
        ),
        name="lloyd_step",
    )(embeddings, centers, assignment.reshape(n_rows // 128, 128))
    return old_min.reshape(n_rows), refined, new_min.reshape(n_rows)


def on_device(embeddings, centers, assignment):
    wide_rows = embeddings.astype(jnp.float32)
    row_norms = jnp.sum(jnp.square(wide_rows), 1)
    starting = jnp.full((embeddings.shape[0],), jnp.inf, jnp.float32)
    portion = lax.all_gather(centers, "shard", axis=0, tiled=True)
    portion_norms = jnp.sum(jnp.square(portion.astype(jnp.float32)), 1)
    products = lax.dot_general(
        embeddings, portion, (((1,), (1,)), ((), ())), preferred_element_type=jnp.float32
    )
    distance = row_norms[:, None] - 2.0 * products + portion_norms[None, :]
    old_min = jnp.minimum(starting, jnp.min(distance, 1))
    n_shard = lax.axis_size("shard")
    owned = centers.shape[0]
    clusters = owned * n_shard
    labels = assignment[:, 0]
    onehot = (labels[:, None] == jnp.arange(clusters, dtype=jnp.int32)[None, :]).astype(
        jnp.bfloat16
    )
    partial_totals = lax.dot_general(
        onehot, embeddings, (((0,), (0,)), ((), ())), preferred_element_type=jnp.float32
    )
    partial_counts = jnp.sum(onehot, 0, dtype=jnp.float32)
    owner_totals, owner_counts = (
        lax.psum_scatter(partial_totals, "shard", scatter_dimension=0, tiled=True),
        lax.psum_scatter(partial_counts, "shard", scatter_dimension=0, tiled=True),
    )
    totals, counts = lax.psum((owner_totals, owner_counts), "grp")
    refined_centers = totals / counts[:, None]
    portion = lax.all_gather(refined_centers, "shard", axis=0, tiled=True)
    portion_norms = jnp.sum(jnp.square(portion), 1)
    products = lax.dot_general(
        wide_rows,
        portion,
        (((1,), (1,)), ((), ())),
        precision=lax.Precision.HIGHEST,
        preferred_element_type=jnp.float32,
    )
    distance = row_norms[:, None] - 2.0 * products + portion_norms[None, :]
    new_min = jnp.minimum(starting, jnp.min(distance, 1))
    return (old_min, refined_centers, new_min)


def solution(mesh):
    placed = (P(("grp", "shard"), None), P("shard", None), P(("grp", "shard"), None))
    here = dict(mesh.shape) == CHIPS
    return jax.shard_map(
        in_one_kernel if here else on_device,
        mesh=mesh,
        in_specs=placed,
        out_specs=(P(("grp", "shard")), P("shard", None), P(("grp", "shard"))),
        check_vma=False,
    )
```

```python
import jax
import jax.numpy as jnp
from jax import lax
from jax.experimental import pallas as pl
from jax.experimental.pallas import tpu as pltpu
from jax.sharding import PartitionSpec as P

MESH = pl.DeviceIdType.MESH
CHIPS = {"grp": 2, "shard": 16}
SLICES = (3, 2, 1, 0)


def dot_nt(left, right):
    return lax.dot_general(
        left, right, (((1,), (1,)), ((), ())), preferred_element_type=jnp.float32
    )


def square_sums(values):
    wide = values.astype(jnp.float32)
    square = wide * wide
    high = square.astype(jnp.bfloat16)
    low = (square - high.astype(jnp.float32)).astype(jnp.bfloat16)
    ones = jnp.ones((16, values.shape[1]), jnp.bfloat16)
    return dot_nt(ones, high) + dot_nt(ones, low)


def column(row):
    return jnp.broadcast_to(row, (128, 128)).T


def pack(block, whole, meta):
    half = whole.shape[1]
    values, count = block[:, 0:half], block[:, half:]
    most = jnp.maximum(jnp.max(jnp.abs(values), 1, keepdims=True), 1e-30)
    whole[...] = jnp.round(values * (32767.0 / most)).astype(jnp.int32).astype(jnp.int16)
    scale = jnp.broadcast_to(most * (1.0 / 32767.0), count.shape)
    lane = lax.broadcasted_iota(jnp.int32, count.shape, 1)
    meta[...] = jnp.where(lane < 4, count, scale).T[0:8]


def unpack(whole, meta):
    half = whole.shape[1]
    count, scale = column(meta[0:1, :]), column(meta[4:5, :])
    values = whole[...].astype(jnp.int32).astype(jnp.float32)
    return jnp.concatenate([values * jnp.concatenate([scale] * (half // 128), 1), count], 1)


def kernel(
    emb, cen, lab, old_out, refined_out, new_out,
    tot, out1, meta1, in1, min1, out2, meta2, in2, min2, out3, meta3, in3, min3,
    rows, labels, old_all, new_all, here, scaled, norms,
    halves, mine, old_acc, new_acc, local_sem, send_sem, recv_sem,
):
    c = lax.axis_index("grp")
    s = lax.axis_index("shard")
    x, y, z = s % 2, (s // 2) % 2, s // 4
    owned, width = cen.shape
    half = width // 2
    n_rows = emb.shape[0]
    x1, y1 = x + (1 - c) * (1 - 2 * x), y + c * (1 - 2 * y)
    x2, y2 = x + c * (1 - 2 * x), y + (1 - c) * (1 - 2 * y)

    def at(zz, yy, xx):
        return zz * 4 + yy * 2 + xx

    def level(j):
        far = (z + 2 * (j // 2)) % 4
        return far + (j % 2) * (1 - 2 * (far % 2))

    sib = (1 - c, s)
    p1 = (c, at(z, y1, x1))
    p2 = (c, at(z, y2, x2))
    above = [None] + [(c, at(level(j), y, x)) for j in (1, 2, 3)]
    cols = pl.ds(pl.multiple_of(c * half, 128), half)
    other_cols = pl.ds(pl.multiple_of((1 - c) * half, 128), half)

    sent = []

    def send(src, dst, device):
        i = len(sent)
        copy = pltpu.make_async_remote_copy(
            src_ref=src, dst_ref=dst, send_sem=send_sem.at[i], recv_sem=recv_sem.at[i],
            device_id=device, device_id_type=MESH,
        )
        copy.start()
        sent.append(copy)
        return copy

    barrier = pltpu.get_barrier_semaphore()
    for peer in (sib, p1, p2, above[1], above[2], above[3]):
        pl.semaphore_signal(barrier, inc=1, device_id=peer, device_id_type=MESH)
    own_lab = pltpu.make_async_copy(lab, labels.at[pl.ds(0, 8)], local_sem.at[3])
    own_lab.start()
    own_emb = pltpu.make_async_copy(emb, here, local_sem.at[4])
    own_emb.start()
    own_rows = pltpu.make_async_copy(emb.at[:, cols], rows.at[0, :, pl.ds(0, half)], local_sem.at[0])
    own_rows.start()
    own_old = pltpu.make_async_copy(cen, old_all.at[s], local_sem.at[1])
    own_old.start()
    rows[:, :, half:] = jnp.ones((2, n_rows, 128), jnp.bfloat16)
    old_acc[...] = jnp.full(old_acc.shape, jnp.inf, jnp.float32)
    new_acc[...] = jnp.full(new_acc.shape, jnp.inf, jnp.float32)
    pl.semaphore_wait(barrier, 6)

    rows_in = send(emb.at[:, other_cols], rows.at[1, :, pl.ds(0, half)], sib)
    labels_in = send(lab, labels.at[pl.ds(8, 8)], sib)

    class Gather:
        def __init__(self, own, buf, share_own):
            self.buf = buf
            spot = buf.at[s, :, cols]
            self.z = [None] + [send(own, spot, above[j]) for j in (1, 2, 3)]
            self.d1 = [send(own, spot, p1)]
            self.d2 = [send(own, spot, p2)]
            self.fz = [send(own, spot, sib) if share_own else None]
            self.f1, self.f2, self.far, self.ffar = [], [], [], []

        def spot(self, j, yy, xx):
            return self.buf.at[at(level(j), yy, xx), :, cols]

        def along_z(self, *which):
            for j in which:
                self.z[j].wait_recv()
                spot = self.spot(j, y, x)
                self.d1.append(send(spot, spot, p1))
                self.d2.append(send(spot, spot, p2))
                self.fz.append(send(spot, spot, sib))

        def along_d1(self, *which):
            for j in which:
                self.d1[j].wait_recv()
                spot = self.spot(j, y1, x1)
                self.far.append(send(spot, spot, p2))
                self.f1.append(send(spot, spot, sib))

        def along_d2(self, *which):
            for j in which:
                self.d2[j].wait_recv()
                spot = self.spot(j, y2, x2)
                self.f2.append(send(spot, spot, sib))

        def last(self, *which):
            for j in which:
                self.far[j].wait_recv()
                spot = self.spot(j, 1 - y, 1 - x)
                self.ffar.append(send(spot, spot, sib))

        def need(self, copies):
            for copy in copies:
                if copy is not None:
                    copy.wait_recv()

    def nearest(buf, acc, yy, xx, start=0, stop=2):
        def pair(i, carry):
            far = (z + 2 * i) % 4
            first = at(far, yy, xx)
            second = at(far + 1 - 2 * (far % 2), yy, xx)
            block = jnp.concatenate([buf[first], buf[second]], 0)
            distance = dot_nt(scaled[...], block) + square_sums(block)[0:1, :]
            near = jnp.minimum(distance[:, :owned], distance[:, owned:])
            acc[...] = jnp.minimum(acc[...], near)
            return carry

        lax.fori_loop(start, stop, pair, 0)

    old = Gather(cen.at[:, cols], old_all, False)

    own_lab.wait()
    own_rows.wait()
    rows_in.wait_recv()
    labels_in.wait_recv()

    def partial(j, fa):
        hot = []
        for fb in range(2):
            xa = x + fa * (x1 - x) + fb * (x2 - x)
            ya = y + fa * (y1 - y) + fb * (y2 - y)
            hot.append(lax.broadcasted_iota(jnp.int32, (owned, 128), 0) + at(level(j), ya, xa) * owned)
        ids = jnp.concatenate(hot, 0)

        def one(g, part):
            hot = [
                (labels[pl.ds(8 * g + r, 1), :] == ids).astype(jnp.float32).astype(jnp.bfloat16)
                for r in range(8)
            ]
            block = jnp.concatenate(hot, 1)
            return part + jnp.dot(block, rows[g], preferred_element_type=jnp.float32)

        part = one(0, jnp.zeros((2 * owned, half + 128), jnp.float32))
        return one(1, part)

    stage1, stage2, stage3 = {}, {}, {}

    def begin(j):
        part = partial(j, 1)
        for fb in range(2):
            pack(part[fb * owned : (fb + 1) * owned], out1.at[j, fb], meta1.at[j, fb])
        stage1[j] = (send(out1.at[j], in1.at[j], p1), send(meta1.at[j], min1.at[j], p1))
        part = partial(j, 0)
        for fb in range(2):
            tot[2 * j + fb] = part[fb * owned : (fb + 1) * owned]

    def middle(j):
        for copy in stage1[j]:
            copy.wait_recv()
        pack(tot[2 * j + 1] + unpack(in1.at[j, 1], min1.at[j, 1]), out2.at[j], meta2.at[j])
        stage2[j] = (send(out2.at[j], in2.at[j], p2), send(meta2.at[j], min2.at[j], p2))
        tot[2 * j] += unpack(in1.at[j, 0], min1.at[j, 0])

    def settle(j):
        for copy in stage2[j]:
            copy.wait_recv()
        tot[2 * j] += unpack(in2.at[j], min2.at[j])
        if j > 0:
            i = j - 1
            pack(tot[2 * j], out3.at[i], meta3.at[i])
            stage3[j] = (send(out3.at[i], in3.at[i], above[j]), send(meta3.at[i], min3.at[i], above[j]))

    begin(SLICES[0])
    begin(SLICES[1])
    old.along_z(1, 2, 3)
    own_emb.wait()
    wide = here[...]
    scaled[...] = wide * jnp.asarray(-2.0, jnp.bfloat16)
    norms[...] = square_sums(wide)[0:8, :]

    middle(SLICES[0])
    begin(SLICES[2])
    middle(SLICES[1])
    settle(SLICES[0])
    begin(SLICES[3])
    middle(SLICES[2])
    settle(SLICES[1])
    old.along_d1(0, 1, 2, 3)
    middle(SLICES[3])
    settle(SLICES[2])
    settle(SLICES[3])
    old.along_d2(0, 1, 2, 3)

    total = tot[0]
    for j in SLICES[:3]:
        for copy in stage3[j]:
            copy.wait_recv()
        total += unpack(in3.at[j - 1], min3.at[j - 1])
    refined = total[:, 0:half] / jnp.concatenate([total[:, half:]] * (half // 128), 1)
    halves[c] = refined
    mine[...] = refined.astype(jnp.bfloat16)
    own_new = pltpu.make_async_copy(mine, new_all.at[s, :, cols], local_sem.at[2])
    own_new.start()
    new = Gather(mine, new_all, True)
    half_in = send(halves.at[c], halves.at[c], sib)

    own_old.wait()
    old.need(old.fz)
    nearest(old_all, old_acc, y, x)
    new.along_z(1)
    old.last(0, 1, 2, 3)
    new.along_z(2)
    old.need(old.f1 + old.f2)
    nearest(old_all, old_acc, y1, x1)
    new.along_z(3)
    new.along_d1(0, 1)
    nearest(old_all, old_acc, y2, x2)
    new.along_d1(2, 3)
    new.along_d2(0, 1, 2, 3)
    old.need(old.ffar)
    nearest(old_all, old_acc, 1 - y, 1 - x)
    new.last(0, 1)
    old_out[...] = jnp.min(old_acc[...].T, 0, keepdims=True) + norms[0:1, :]
    half_in.wait_recv()
    refined_out[:, 0:half] = halves[0]
    refined_out[:, half:width] = halves[1]
    own_new.wait()
    new.need(new.fz)
    nearest(new_all, new_acc, y, x)
    new.last(2, 3)
    new.need(new.f1 + new.f2)
    nearest(new_all, new_acc, y1, x1)
    nearest(new_all, new_acc, y2, x2)
    new.need(new.ffar[:2])
    nearest(new_all, new_acc, 1 - y, 1 - x, 0, 1)
    new.need(new.ffar[2:])
    nearest(new_all, new_acc, 1 - y, 1 - x, 1, 2)
    new_out[...] = jnp.min(new_acc[...].T, 0, keepdims=True) + norms[0:1, :]
    for copy in sent:
        copy.wait_send()


COPIES = 96


def write_out(old_min, refined, new_min, old_out, refined_out, new_out, sems):
    pairs = ((old_min, old_out), (refined, refined_out), (new_min, new_out))
    copies = [pltpu.make_async_copy(src, dst, sems.at[i]) for i, (src, dst) in enumerate(pairs)]
    for copy in copies:
        copy.start()
    for copy in copies:
        copy.wait()


def in_one_kernel(embeddings, centers, assignment):
    n_rows, width = embeddings.shape
    owned = centers.shape[0]
    half = width // 2
    f32, bf16, i16 = jnp.float32, jnp.bfloat16, jnp.int16
    vmem = pl.BlockSpec(memory_space=pltpu.VMEM)
    old_min, refined, new_min = pl.pallas_call(
        kernel,
        out_shape=(
            jax.ShapeDtypeStruct((1, n_rows), f32),
            jax.ShapeDtypeStruct((owned, width), f32),
            jax.ShapeDtypeStruct((1, n_rows), f32),
        ),
        in_specs=[pl.BlockSpec(memory_space=pl.ANY)] * 3,
        out_specs=(vmem,) * 3,
        scratch_shapes=[
            pltpu.VMEM((8, owned, half + 128), f32),
            pltpu.VMEM((4, 2, owned, half), i16),
            pltpu.VMEM((4, 2, 8, 128), f32),
            pltpu.VMEM((4, 2, owned, half), i16),
            pltpu.VMEM((4, 2, 8, 128), f32),
            pltpu.VMEM((4, owned, half), i16),
            pltpu.VMEM((4, 8, 128), f32),
            pltpu.VMEM((4, owned, half), i16),
            pltpu.VMEM((4, 8, 128), f32),
            pltpu.VMEM((3, owned, half), i16),
            pltpu.VMEM((3, 8, 128), f32),
            pltpu.VMEM((3, owned, half), i16),
            pltpu.VMEM((3, 8, 128), f32),
            pltpu.VMEM((2, n_rows, half + 128), bf16),
            pltpu.VMEM((16, 128), jnp.int32),
            pltpu.VMEM((16, owned, width), bf16),
            pltpu.VMEM((16, owned, width), bf16),
            pltpu.VMEM((n_rows, width), bf16),
            pltpu.VMEM((n_rows, width), bf16),
            pltpu.VMEM((8, n_rows), f32),
            pltpu.VMEM((2, owned, half), f32),
            pltpu.VMEM((owned, half), bf16),
            pltpu.VMEM((n_rows, owned), f32),
            pltpu.VMEM((n_rows, owned), f32),
            pltpu.SemaphoreType.DMA((5,)),
            pltpu.SemaphoreType.DMA((COPIES,)),
            pltpu.SemaphoreType.DMA((COPIES,)),
        ],
        compiler_params=pltpu.CompilerParams(
            collective_id=0, has_side_effects=True, vmem_limit_bytes=60 * 1024 * 1024
        ),
        cost_estimate=pl.CostEstimate(
            flops=6 * n_rows * 16 * owned * width, bytes_accessed=8 * n_rows * width, transcendentals=0
        ),
        name="lloyd_step",
    )(embeddings, centers, assignment.reshape(n_rows // 128, 128))
    outs = (old_min, refined, new_min)
    anywhere = pl.BlockSpec(memory_space=pl.ANY)
    old_min, refined, new_min = pl.pallas_call(
        write_out,
        out_shape=tuple(jax.ShapeDtypeStruct(out.shape, f32) for out in outs),
        in_specs=[anywhere] * 3,
        out_specs=(anywhere,) * 3,
        scratch_shapes=[pltpu.SemaphoreType.DMA((3,))],
        compiler_params=pltpu.CompilerParams(vmem_limit_bytes=60 * 1024 * 1024),
        name="write_out",
    )(*outs)
    return old_min.reshape(n_rows), refined, new_min.reshape(n_rows)


def on_device(embeddings, centers, assignment):
    wide_rows = embeddings.astype(jnp.float32)
    row_norms = jnp.sum(jnp.square(wide_rows), 1)
    starting = jnp.full((embeddings.shape[0],), jnp.inf, jnp.float32)
    portion = lax.all_gather(centers, "shard", axis=0, tiled=True)
    portion_norms = jnp.sum(jnp.square(portion.astype(jnp.float32)), 1)
    products = lax.dot_general(
        embeddings, portion, (((1,), (1,)), ((), ())), preferred_element_type=jnp.float32
    )
    distance = row_norms[:, None] - 2.0 * products + portion_norms[None, :]
    old_min = jnp.minimum(starting, jnp.min(distance, 1))
    n_shard = lax.axis_size("shard")
    owned = centers.shape[0]
    clusters = owned * n_shard
    labels = assignment[:, 0]
    onehot = (labels[:, None] == jnp.arange(clusters, dtype=jnp.int32)[None, :]).astype(
        jnp.bfloat16
    )
    partial_totals = lax.dot_general(
        onehot, embeddings, (((0,), (0,)), ((), ())), preferred_element_type=jnp.float32
    )
    partial_counts = jnp.sum(onehot, 0, dtype=jnp.float32)
    owner_totals, owner_counts = (
        lax.psum_scatter(partial_totals, "shard", scatter_dimension=0, tiled=True),
        lax.psum_scatter(partial_counts, "shard", scatter_dimension=0, tiled=True),
    )
    totals, counts = lax.psum((owner_totals, owner_counts), "grp")
    refined_centers = totals / counts[:, None]
    portion = lax.all_gather(refined_centers, "shard", axis=0, tiled=True)
    portion_norms = jnp.sum(jnp.square(portion), 1)
    products = lax.dot_general(
        wide_rows,
        portion,
        (((1,), (1,)), ((), ())),
        precision=lax.Precision.HIGHEST,
        preferred_element_type=jnp.float32,
    )
    distance = row_norms[:, None] - 2.0 * products + portion_norms[None, :]
    new_min = jnp.minimum(starting, jnp.min(distance, 1))
    return (old_min, refined_centers, new_min)


def solution(mesh):
    placed = (P(("grp", "shard"), None), P("shard", None), P(("grp", "shard"), None))
    here = dict(mesh.shape) == CHIPS
    return jax.shard_map(
        in_one_kernel if here else on_device,
        mesh=mesh,
        in_specs=placed,
        out_specs=(P(("grp", "shard")), P("shard", None), P(("grp", "shard"))),
        check_vma=False,
    )
```

```python
import jax
import jax.numpy as jnp
from jax import lax
from jax.experimental import pallas as pl
from jax.experimental.pallas import tpu as pltpu
from jax.sharding import PartitionSpec as P

MESH = pl.DeviceIdType.MESH
CHIPS = {"grp": 2, "shard": 16}
SLICES = (3, 2, 1, 0)


def dot_nt(left, right):
    return lax.dot_general(
        left, right, (((1,), (1,)), ((), ())), preferred_element_type=jnp.float32
    )


def square_sums(values):
    wide = values.astype(jnp.float32)
    square = wide * wide
    high = square.astype(jnp.bfloat16)
    low = (square - high.astype(jnp.float32)).astype(jnp.bfloat16)
    ones = jnp.ones((16, values.shape[1]), jnp.bfloat16)
    return dot_nt(ones, high) + dot_nt(ones, low)


def column(row):
    return jnp.broadcast_to(row, (128, 128)).T


def pack(block, whole, meta):
    half = whole.shape[1]
    values, count = block[:, 0:half], block[:, half:]
    most = jnp.maximum(jnp.max(jnp.abs(values), 1, keepdims=True), 1e-30)
    whole[...] = jnp.round(values * (32767.0 / most)).astype(jnp.int32).astype(jnp.int16)
    scale = jnp.broadcast_to(most * (1.0 / 32767.0), count.shape)
    lane = lax.broadcasted_iota(jnp.int32, count.shape, 1)
    meta[...] = jnp.where(lane < 4, count, scale).T[0:8]


def unpack(whole, meta):
    half = whole.shape[1]
    count, scale = column(meta[0:1, :]), column(meta[4:5, :])
    values = whole[...].astype(jnp.int32).astype(jnp.float32)
    return jnp.concatenate([values * jnp.concatenate([scale] * (half // 128), 1), count], 1)


def kernel(
    emb, cen, lab, old_out, refined_out, new_out,
    tot, out1, meta1, in1, min1, out2, meta2, in2, min2, out3, meta3, in3, min3,
    rows, labels, old_all, new_all, here, scaled, norms,
    halves, mine, old_acc, new_acc, local_sem, send_sem, recv_sem,
):
    c = lax.axis_index("grp")
    s = lax.axis_index("shard")
    x, y, z = s % 2, (s // 2) % 2, s // 4
    owned, width = cen.shape
    half = width // 2
    n_rows = emb.shape[0]
    x1, y1 = x + (1 - c) * (1 - 2 * x), y + c * (1 - 2 * y)
    x2, y2 = x + c * (1 - 2 * x), y + (1 - c) * (1 - 2 * y)

    def at(zz, yy, xx):
        return zz * 4 + yy * 2 + xx

    def level(j):
        far = (z + 2 * (j // 2)) % 4
        return far + (j % 2) * (1 - 2 * (far % 2))

    sib = (1 - c, s)
    p1 = (c, at(z, y1, x1))
    p2 = (c, at(z, y2, x2))
    above = [None] + [(c, at(level(j), y, x)) for j in (1, 2, 3)]
    cols = pl.ds(pl.multiple_of(c * half, 128), half)
    other_cols = pl.ds(pl.multiple_of((1 - c) * half, 128), half)

    sent = []

    def send(src, dst, device):
        i = len(sent)
        copy = pltpu.make_async_remote_copy(
            src_ref=src, dst_ref=dst, send_sem=send_sem.at[i], recv_sem=recv_sem.at[i],
            device_id=device, device_id_type=MESH,
        )
        copy.start()
        sent.append(copy)
        return copy

    barrier = pltpu.get_barrier_semaphore()
    for peer in (sib, p1, p2, above[1], above[2], above[3]):
        pl.semaphore_signal(barrier, inc=1, device_id=peer, device_id_type=MESH)
    own_lab = pltpu.make_async_copy(lab, labels.at[pl.ds(0, 8)], local_sem.at[3])
    own_lab.start()
    own_emb = pltpu.make_async_copy(emb, here, local_sem.at[4])
    own_emb.start()
    own_rows = pltpu.make_async_copy(emb.at[:, cols], rows.at[0, :, pl.ds(0, half)], local_sem.at[0])
    own_rows.start()
    own_old = pltpu.make_async_copy(cen, old_all.at[s], local_sem.at[1])
    own_old.start()
    rows[:, :, half:] = jnp.ones((2, n_rows, 128), jnp.bfloat16)
    old_acc[...] = jnp.full(old_acc.shape, jnp.inf, jnp.float32)
    new_acc[...] = jnp.full(new_acc.shape, jnp.inf, jnp.float32)
    pl.semaphore_wait(barrier, 6)

    rows_in = send(emb.at[:, other_cols], rows.at[1, :, pl.ds(0, half)], sib)
    labels_in = send(lab, labels.at[pl.ds(8, 8)], sib)

    class Gather:
        def __init__(self, own, buf, share_own):
            self.buf = buf
            spot = buf.at[s, :, cols]
            self.z = [None] + [send(own, spot, above[j]) for j in (1, 2, 3)]
            self.d1 = [send(own, spot, p1)]
            self.d2 = [send(own, spot, p2)]
            self.fz = [send(own, spot, sib) if share_own else None]
            self.f1, self.f2, self.far, self.ffar = [], [], [], []

        def spot(self, j, yy, xx):
            return self.buf.at[at(level(j), yy, xx), :, cols]

        def along_z(self, *which):
            for j in which:
                self.z[j].wait_recv()
                spot = self.spot(j, y, x)
                self.d1.append(send(spot, spot, p1))
                self.d2.append(send(spot, spot, p2))
                self.fz.append(send(spot, spot, sib))

        def along_d1(self, *which):
            for j in which:
                self.d1[j].wait_recv()
                spot = self.spot(j, y1, x1)
                self.far.append(send(spot, spot, p2))
                self.f1.append(send(spot, spot, sib))

        def along_d2(self, *which):
            for j in which:
                self.d2[j].wait_recv()
                spot = self.spot(j, y2, x2)
                self.f2.append(send(spot, spot, sib))

        def last(self, *which):
            for j in which:
                self.far[j].wait_recv()
                spot = self.spot(j, 1 - y, 1 - x)
                self.ffar.append(send(spot, spot, sib))

        def need(self, copies):
            for copy in copies:
                if copy is not None:
                    copy.wait_recv()

    def nearest(buf, acc, yy, xx, start=0, stop=2):
        def pair(i, carry):
            far = (z + 2 * i) % 4
            first = at(far, yy, xx)
            second = at(far + 1 - 2 * (far % 2), yy, xx)
            block = jnp.concatenate([buf[first], buf[second]], 0)
            distance = dot_nt(scaled[...], block) + square_sums(block)[0:1, :]
            near = jnp.minimum(distance[:, :owned], distance[:, owned:])
            acc[...] = jnp.minimum(acc[...], near)
            return carry

        lax.fori_loop(start, stop, pair, 0)

    old = Gather(cen.at[:, cols], old_all, False)

    own_lab.wait()
    own_rows.wait()
    old.along_z(1)

    def partial(j, fa, first=False):
        hot = []
        for fb in range(2):
            xa = x + fa * (x1 - x) + fb * (x2 - x)
            ya = y + fa * (y1 - y) + fb * (y2 - y)
            hot.append(lax.broadcasted_iota(jnp.int32, (owned, 128), 0) + at(level(j), ya, xa) * owned)
        ids = jnp.concatenate(hot, 0)

        def one(g, part):
            hot = [
                (labels[pl.ds(8 * g + r, 1), :] == ids).astype(jnp.float32).astype(jnp.bfloat16)
                for r in range(8)
            ]
            block = jnp.concatenate(hot, 1)
            return part + jnp.dot(block, rows[g], preferred_element_type=jnp.float32)

        part = one(0, jnp.zeros((2 * owned, half + 128), jnp.float32))
        if first:
            rows_in.wait_recv()
            labels_in.wait_recv()
        return one(1, part)

    stage1, stage2, stage3 = {}, {}, {}

    def begin(j):
        part = partial(j, 1, j == SLICES[0])
        for fb in range(2):
            pack(part[fb * owned : (fb + 1) * owned], out1.at[j, fb], meta1.at[j, fb])
        stage1[j] = (send(out1.at[j], in1.at[j], p1), send(meta1.at[j], min1.at[j], p1))
        part = partial(j, 0)
        for fb in range(2):
            tot[2 * j + fb] = part[fb * owned : (fb + 1) * owned]

    def middle(j):
        for copy in stage1[j]:
            copy.wait_recv()
        pack(tot[2 * j + 1] + unpack(in1.at[j, 1], min1.at[j, 1]), out2.at[j], meta2.at[j])
        stage2[j] = (send(out2.at[j], in2.at[j], p2), send(meta2.at[j], min2.at[j], p2))
        tot[2 * j] += unpack(in1.at[j, 0], min1.at[j, 0])

    def settle(j):
        for copy in stage2[j]:
            copy.wait_recv()
        tot[2 * j] += unpack(in2.at[j], min2.at[j])
        if j > 0:
            i = j - 1
            pack(tot[2 * j], out3.at[i], meta3.at[i])
            stage3[j] = (send(out3.at[i], in3.at[i], above[j]), send(meta3.at[i], min3.at[i], above[j]))

    begin(SLICES[0])
    old.along_z(2, 3)
    begin(SLICES[1])
    middle(SLICES[0])
    own_emb.wait()
    wide = here[...]
    scaled[...] = wide * jnp.asarray(-2.0, jnp.bfloat16)
    norms[...] = square_sums(wide)[0:8, :]

    begin(SLICES[2])
    middle(SLICES[1])
    settle(SLICES[0])
    old.along_d1(0, 1)
    begin(SLICES[3])
    middle(SLICES[2])
    settle(SLICES[1])
    old.along_d1(2, 3)
    middle(SLICES[3])
    settle(SLICES[2])
    own_old.wait()
    old.need(old.fz)
    nearest(old_all, old_acc, y, x)
    old.along_d2(0, 1, 2, 3)
    settle(SLICES[3])

    total = tot[0]
    for j in SLICES[:3]:
        for copy in stage3[j]:
            copy.wait_recv()
        total += unpack(in3.at[j - 1], min3.at[j - 1])
    refined = total[:, 0:half] / jnp.concatenate([total[:, half:]] * (half // 128), 1)
    halves[c] = refined
    mine[...] = refined.astype(jnp.bfloat16)
    own_new = pltpu.make_async_copy(mine, new_all.at[s, :, cols], local_sem.at[2])
    own_new.start()
    new = Gather(mine, new_all, True)
    half_in = send(halves.at[c], halves.at[c], sib)

    new.along_z(1)
    old.last(0, 1, 2, 3)
    new.along_z(2)
    old.need(old.f1 + old.f2)
    nearest(old_all, old_acc, y1, x1)
    new.along_z(3)
    new.along_d1(0, 1)
    nearest(old_all, old_acc, y2, x2)
    new.along_d1(2, 3)
    new.along_d2(0, 1, 2, 3)
    old.need(old.ffar)
    nearest(old_all, old_acc, 1 - y, 1 - x)
    new.last(0, 1)
    old_out[...] = jnp.min(old_acc[...].T, 0, keepdims=True) + norms[0:1, :]
    half_in.wait_recv()
    refined_out[:, 0:half] = halves[0]
    refined_out[:, half:width] = halves[1]
    own_new.wait()
    new.need(new.fz)
    nearest(new_all, new_acc, y, x)
    new.last(2, 3)
    new.need(new.f1 + new.f2)
    nearest(new_all, new_acc, y1, x1)
    nearest(new_all, new_acc, y2, x2)
    new.need(new.ffar[:2])
    nearest(new_all, new_acc, 1 - y, 1 - x, 0, 1)
    new.need(new.ffar[2:])
    nearest(new_all, new_acc, 1 - y, 1 - x, 1, 2)
    new_out[...] = jnp.min(new_acc[...].T, 0, keepdims=True) + norms[0:1, :]
    for copy in sent:
        copy.wait_send()


COPIES = 96


def in_one_kernel(embeddings, centers, assignment):
    n_rows, width = embeddings.shape
    owned = centers.shape[0]
    half = width // 2
    f32, bf16, i16 = jnp.float32, jnp.bfloat16, jnp.int16
    vmem = pl.BlockSpec(memory_space=pltpu.VMEM)
    old_min, refined, new_min = pl.pallas_call(
        kernel,
        out_shape=(
            jax.ShapeDtypeStruct((1, n_rows), f32),
            jax.ShapeDtypeStruct((owned, width), f32),
            jax.ShapeDtypeStruct((1, n_rows), f32),
        ),
        in_specs=[pl.BlockSpec(memory_space=pl.ANY)] * 3,
        out_specs=(vmem,) * 3,
        scratch_shapes=[
            pltpu.VMEM((8, owned, half + 128), f32),
            pltpu.VMEM((4, 2, owned, half), i16),
            pltpu.VMEM((4, 2, 8, 128), f32),
            pltpu.VMEM((4, 2, owned, half), i16),
            pltpu.VMEM((4, 2, 8, 128), f32),
            pltpu.VMEM((4, owned, half), i16),
            pltpu.VMEM((4, 8, 128), f32),
            pltpu.VMEM((4, owned, half), i16),
            pltpu.VMEM((4, 8, 128), f32),
            pltpu.VMEM((3, owned, half), i16),
            pltpu.VMEM((3, 8, 128), f32),
            pltpu.VMEM((3, owned, half), i16),
            pltpu.VMEM((3, 8, 128), f32),
            pltpu.VMEM((2, n_rows, half + 128), bf16),
            pltpu.VMEM((16, 128), jnp.int32),
            pltpu.VMEM((16, owned, width), bf16),
            pltpu.VMEM((16, owned, width), bf16),
            pltpu.VMEM((n_rows, width), bf16),
            pltpu.VMEM((n_rows, width), bf16),
            pltpu.VMEM((8, n_rows), f32),
            pltpu.VMEM((2, owned, half), f32),
            pltpu.VMEM((owned, half), bf16),
            pltpu.VMEM((n_rows, owned), f32),
            pltpu.VMEM((n_rows, owned), f32),
            pltpu.SemaphoreType.DMA((5,)),
            pltpu.SemaphoreType.DMA((COPIES,)),
            pltpu.SemaphoreType.DMA((COPIES,)),
        ],
        compiler_params=pltpu.CompilerParams(
            collective_id=0, has_side_effects=True, vmem_limit_bytes=60 * 1024 * 1024
        ),
        cost_estimate=pl.CostEstimate(
            flops=6 * n_rows * 16 * owned * width, bytes_accessed=8 * n_rows * width, transcendentals=0
        ),
        name="lloyd_step",
    )(embeddings, centers, assignment.reshape(n_rows // 128, 128))
    return old_min.reshape(n_rows), refined, new_min.reshape(n_rows)


def on_device(embeddings, centers, assignment):
    wide_rows = embeddings.astype(jnp.float32)
    row_norms = jnp.sum(jnp.square(wide_rows), 1)
    starting = jnp.full((embeddings.shape[0],), jnp.inf, jnp.float32)
    portion = lax.all_gather(centers, "shard", axis=0, tiled=True)
    portion_norms = jnp.sum(jnp.square(portion.astype(jnp.float32)), 1)
    products = lax.dot_general(
        embeddings, portion, (((1,), (1,)), ((), ())), preferred_element_type=jnp.float32
    )
    distance = row_norms[:, None] - 2.0 * products + portion_norms[None, :]
    old_min = jnp.minimum(starting, jnp.min(distance, 1))
    n_shard = lax.axis_size("shard")
    owned = centers.shape[0]
    clusters = owned * n_shard
    labels = assignment[:, 0]
    onehot = (labels[:, None] == jnp.arange(clusters, dtype=jnp.int32)[None, :]).astype(
        jnp.bfloat16
    )
    partial_totals = lax.dot_general(
        onehot, embeddings, (((0,), (0,)), ((), ())), preferred_element_type=jnp.float32
    )
    partial_counts = jnp.sum(onehot, 0, dtype=jnp.float32)
    owner_totals, owner_counts = (
        lax.psum_scatter(partial_totals, "shard", scatter_dimension=0, tiled=True),
        lax.psum_scatter(partial_counts, "shard", scatter_dimension=0, tiled=True),
    )
    totals, counts = lax.psum((owner_totals, owner_counts), "grp")
    refined_centers = totals / counts[:, None]
    portion = lax.all_gather(refined_centers, "shard", axis=0, tiled=True)
    portion_norms = jnp.sum(jnp.square(portion), 1)
    products = lax.dot_general(
        wide_rows,
        portion,
        (((1,), (1,)), ((), ())),
        precision=lax.Precision.HIGHEST,
        preferred_element_type=jnp.float32,
    )
    distance = row_norms[:, None] - 2.0 * products + portion_norms[None, :]
    new_min = jnp.minimum(starting, jnp.min(distance, 1))
    return (old_min, refined_centers, new_min)


def solution(mesh):
    placed = (P(("grp", "shard"), None), P("shard", None), P(("grp", "shard"), None))
    here = dict(mesh.shape) == CHIPS
    return jax.shard_map(
        in_one_kernel if here else on_device,
        mesh=mesh,
        in_specs=placed,
        out_specs=(P(("grp", "shard")), P("shard", None), P(("grp", "shard"))),
        check_vma=False,
    )
```

```python
import jax
import jax.numpy as jnp
from jax import lax
from jax.experimental import pallas as pl
from jax.experimental.pallas import tpu as pltpu
from jax.sharding import PartitionSpec as P

MESH = pl.DeviceIdType.MESH
CHIPS = {"grp": 2, "shard": 16}
SLICES = (3, 2, 1, 0)


def dot_nt(left, right):
    return lax.dot_general(
        left, right, (((1,), (1,)), ((), ())), preferred_element_type=jnp.float32
    )


def square_sums(values):
    wide = values.astype(jnp.float32)
    square = wide * wide
    high = square.astype(jnp.bfloat16)
    low = (square - high.astype(jnp.float32)).astype(jnp.bfloat16)
    ones = jnp.ones((16, values.shape[1]), jnp.bfloat16)
    return dot_nt(ones, high) + dot_nt(ones, low)


def column(row):
    return jnp.broadcast_to(row, (128, 128)).T


def pack(block, whole, meta):
    half = whole.shape[1]
    values, count = block[:, 0:half], block[:, half:]
    most = jnp.maximum(jnp.max(jnp.abs(values), 1, keepdims=True), 1e-30)
    whole[...] = jnp.round(values * (32767.0 / most)).astype(jnp.int32).astype(jnp.int16)
    scale = jnp.broadcast_to(most * (1.0 / 32767.0), count.shape)
    lane = lax.broadcasted_iota(jnp.int32, count.shape, 1)
    meta[...] = jnp.where(lane < 4, count, scale).T[0:8]


def unpack(whole, meta):
    half = whole.shape[1]
    count, scale = column(meta[0:1, :]), column(meta[4:5, :])
    values = whole[...].astype(jnp.int32).astype(jnp.float32)
    return jnp.concatenate([values * jnp.concatenate([scale] * (half // 128), 1), count], 1)


def kernel(
    emb, cen, lab, old_out, refined_out, new_out,
    tot, out1, meta1, in1, min1, out2, meta2, in2, min2, out3, meta3, in3, min3,
    rows, labels, old_all, new_all, here, scaled, norms,
    halves, mine, old_acc, new_acc, local_sem, send_sem, recv_sem,
):
    c = lax.axis_index("grp")
    s = lax.axis_index("shard")
    x, y, z = s % 2, (s // 2) % 2, s // 4
    owned, width = cen.shape
    half = width // 2
    n_rows = emb.shape[0]
    x1, y1 = x + (1 - c) * (1 - 2 * x), y + c * (1 - 2 * y)
    x2, y2 = x + c * (1 - 2 * x), y + (1 - c) * (1 - 2 * y)

    def at(zz, yy, xx):
        return zz * 4 + yy * 2 + xx

    def level(j):
        far = (z + 2 * (j // 2)) % 4
        return far + (j % 2) * (1 - 2 * (far % 2))

    sib = (1 - c, s)
    p1 = (c, at(z, y1, x1))
    p2 = (c, at(z, y2, x2))
    above = [None] + [(c, at(level(j), y, x)) for j in (1, 2, 3)]
    cols = pl.ds(pl.multiple_of(c * half, 128), half)
    other_cols = pl.ds(pl.multiple_of((1 - c) * half, 128), half)

    sent = []

    def send(src, dst, device):
        i = len(sent)
        copy = pltpu.make_async_remote_copy(
            src_ref=src, dst_ref=dst, send_sem=send_sem.at[i], recv_sem=recv_sem.at[i],
            device_id=device, device_id_type=MESH,
        )
        copy.start()
        sent.append(copy)
        return copy

    barrier = pltpu.get_barrier_semaphore()
    for peer in (sib, p1, p2, above[1], above[2], above[3]):
        pl.semaphore_signal(barrier, inc=1, device_id=peer, device_id_type=MESH)
    own_lab = pltpu.make_async_copy(lab, labels.at[pl.ds(0, 8)], local_sem.at[3])
    own_lab.start()
    own_emb = pltpu.make_async_copy(emb, here, local_sem.at[4])
    own_emb.start()
    own_rows = pltpu.make_async_copy(emb.at[:, cols], rows.at[0, :, pl.ds(0, half)], local_sem.at[0])
    own_rows.start()
    own_old = pltpu.make_async_copy(cen, old_all.at[s], local_sem.at[1])
    own_old.start()
    rows[:, :, half:] = jnp.ones((2, n_rows, 128), jnp.bfloat16)
    old_acc[...] = jnp.full(old_acc.shape, jnp.inf, jnp.float32)
    new_acc[...] = jnp.full(new_acc.shape, jnp.inf, jnp.float32)
    pl.semaphore_wait(barrier, 6)

    rows_in = send(emb.at[:, other_cols], rows.at[1, :, pl.ds(0, half)], sib)
    labels_in = send(lab, labels.at[pl.ds(8, 8)], sib)

    class Gather:
        def __init__(self, own, buf, share_own):
            self.buf = buf
            spot = buf.at[s, :, cols]
            self.z = [None] + [send(own, spot, above[j]) for j in (1, 2, 3)]
            self.d1 = [send(own, spot, p1)]
            self.d2 = [send(own, spot, p2)]
            self.fz = [send(own, spot, sib) if share_own else None]
            self.f1, self.f2, self.far, self.ffar = [], [], [], []

        def spot(self, j, yy, xx):
            return self.buf.at[at(level(j), yy, xx), :, cols]

        def along_z(self, *which):
            for j in which:
                self.z[j].wait_recv()
                spot = self.spot(j, y, x)
                self.d1.append(send(spot, spot, p1))
                self.d2.append(send(spot, spot, p2))
                self.fz.append(send(spot, spot, sib))

        def along_d1(self, *which):
            for j in which:
                self.d1[j].wait_recv()
                spot = self.spot(j, y1, x1)
                self.far.append(send(spot, spot, p2))
                self.f1.append(send(spot, spot, sib))

        def along_d2(self, *which):
            for j in which:
                self.d2[j].wait_recv()
                spot = self.spot(j, y2, x2)
                self.f2.append(send(spot, spot, sib))

        def last(self, *which):
            for j in which:
                self.far[j].wait_recv()
                spot = self.spot(j, 1 - y, 1 - x)
                self.ffar.append(send(spot, spot, sib))

        def need(self, copies):
            for copy in copies:
                if copy is not None:
                    copy.wait_recv()

    def nearest(buf, acc, yy, xx, start=0, stop=2):
        def pair(i, carry):
            far = (z + 2 * i) % 4
            first = at(far, yy, xx)
            second = at(far + 1 - 2 * (far % 2), yy, xx)
            block = jnp.concatenate([buf[first], buf[second]], 0)
            distance = dot_nt(scaled[...], block) + square_sums(block)[0:1, :]
            near = jnp.minimum(distance[:, :owned], distance[:, owned:])
            acc[...] = jnp.minimum(acc[...], near)
            return carry

        lax.fori_loop(start, stop, pair, 0)

    old = Gather(cen.at[:, cols], old_all, False)

    own_lab.wait()
    own_rows.wait()

    def partial(j, fa, first=False):
        hot = []
        for fb in range(2):
            xa = x + fa * (x1 - x) + fb * (x2 - x)
            ya = y + fa * (y1 - y) + fb * (y2 - y)
            hot.append(lax.broadcasted_iota(jnp.int32, (owned, 128), 0) + at(level(j), ya, xa) * owned)
        ids = jnp.concatenate(hot, 0)

        def one(g, part):
            hot = [
                (labels[pl.ds(8 * g + r, 1), :] == ids).astype(jnp.float32).astype(jnp.bfloat16)
                for r in range(8)
            ]
            block = jnp.concatenate(hot, 1)
            return part + jnp.dot(block, rows[g], preferred_element_type=jnp.float32)

        part = one(0, jnp.zeros((2 * owned, half + 128), jnp.float32))
        if first:
            rows_in.wait_recv()
            labels_in.wait_recv()
        return one(1, part)

    stage1, stage2, stage3 = {}, {}, {}

    def begin(j):
        part = partial(j, 1, j == SLICES[0])
        for fb in range(2):
            pack(part[fb * owned : (fb + 1) * owned], out1.at[j, fb], meta1.at[j, fb])
        stage1[j] = (send(out1.at[j], in1.at[j], p1), send(meta1.at[j], min1.at[j], p1))
        part = partial(j, 0)
        for fb in range(2):
            tot[2 * j + fb] = part[fb * owned : (fb + 1) * owned]

    def middle(j):
        for copy in stage1[j]:
            copy.wait_recv()
        pack(tot[2 * j + 1] + unpack(in1.at[j, 1], min1.at[j, 1]), out2.at[j], meta2.at[j])
        stage2[j] = (send(out2.at[j], in2.at[j], p2), send(meta2.at[j], min2.at[j], p2))
        tot[2 * j] += unpack(in1.at[j, 0], min1.at[j, 0])

    def settle(j):
        for copy in stage2[j]:
            copy.wait_recv()
        tot[2 * j] += unpack(in2.at[j], min2.at[j])
        if j > 0:
            i = j - 1
            pack(tot[2 * j], out3.at[i], meta3.at[i])
            stage3[j] = (send(out3.at[i], in3.at[i], above[j]), send(meta3.at[i], min3.at[i], above[j]))

    begin(SLICES[0])
    begin(SLICES[1])
    old.along_z(1, 2, 3)
    middle(SLICES[0])
    own_emb.wait()
    wide = here[...]
    scaled[...] = wide * jnp.asarray(-2.0, jnp.bfloat16)
    norms[...] = square_sums(wide)[0:8, :]

    begin(SLICES[2])
    middle(SLICES[1])
    settle(SLICES[0])
    begin(SLICES[3])
    middle(SLICES[2])
    settle(SLICES[1])
    old.along_d1(0, 1, 2, 3)
    middle(SLICES[3])
    settle(SLICES[2])
    own_old.wait()
    old.need(old.fz)
    nearest(old_all, old_acc, y, x)
    settle(SLICES[3])
    old.along_d2(0, 1, 2, 3)

    total = tot[0]
    for j in SLICES[:3]:
        for copy in stage3[j]:
            copy.wait_recv()
        total += unpack(in3.at[j - 1], min3.at[j - 1])
    refined = total[:, 0:half] / jnp.concatenate([total[:, half:]] * (half // 128), 1)
    halves[c] = refined
    mine[...] = refined.astype(jnp.bfloat16)
    own_new = pltpu.make_async_copy(mine, new_all.at[s, :, cols], local_sem.at[2])
    own_new.start()
    new = Gather(mine, new_all, True)
    half_in = send(halves.at[c], halves.at[c], sib)

    new.along_z(1)
    old.last(0, 1, 2, 3)
    new.along_z(2)
    old.need(old.f1 + old.f2)
    nearest(old_all, old_acc, y1, x1)
    new.along_z(3)
    new.along_d1(0, 1)
    nearest(old_all, old_acc, y2, x2)
    new.along_d1(2, 3)
    new.along_d2(0, 1, 2, 3)
    old.need(old.ffar)
    nearest(old_all, old_acc, 1 - y, 1 - x)
    new.last(0, 1)
    old_out[...] = jnp.min(old_acc[...].T, 0, keepdims=True) + norms[0:1, :]
    half_in.wait_recv()
    refined_out[:, 0:half] = halves[0]
    refined_out[:, half:width] = halves[1]
    own_new.wait()
    new.need(new.fz)
    nearest(new_all, new_acc, y, x)
    new.last(2, 3)
    new.need(new.f1 + new.f2)
    nearest(new_all, new_acc, y1, x1)
    nearest(new_all, new_acc, y2, x2)
    new.need(new.ffar[:2])
    nearest(new_all, new_acc, 1 - y, 1 - x, 0, 1)
    new.need(new.ffar[2:])
    nearest(new_all, new_acc, 1 - y, 1 - x, 1, 2)
    new_out[...] = jnp.min(new_acc[...].T, 0, keepdims=True) + norms[0:1, :]
    for copy in sent:
        copy.wait_send()


COPIES = 96


def in_one_kernel(embeddings, centers, assignment):
    n_rows, width = embeddings.shape
    owned = centers.shape[0]
    half = width // 2
    f32, bf16, i16 = jnp.float32, jnp.bfloat16, jnp.int16
    vmem = pl.BlockSpec(memory_space=pltpu.VMEM)
    old_min, refined, new_min = pl.pallas_call(
        kernel,
        out_shape=(
            jax.ShapeDtypeStruct((1, n_rows), f32),
            jax.ShapeDtypeStruct((owned, width), f32),
            jax.ShapeDtypeStruct((1, n_rows), f32),
        ),
        in_specs=[pl.BlockSpec(memory_space=pl.ANY)] * 3,
        out_specs=(vmem,) * 3,
        scratch_shapes=[
            pltpu.VMEM((8, owned, half + 128), f32),
            pltpu.VMEM((4, 2, owned, half), i16),
            pltpu.VMEM((4, 2, 8, 128), f32),
            pltpu.VMEM((4, 2, owned, half), i16),
            pltpu.VMEM((4, 2, 8, 128), f32),
            pltpu.VMEM((4, owned, half), i16),
            pltpu.VMEM((4, 8, 128), f32),
            pltpu.VMEM((4, owned, half), i16),
            pltpu.VMEM((4, 8, 128), f32),
            pltpu.VMEM((3, owned, half), i16),
            pltpu.VMEM((3, 8, 128), f32),
            pltpu.VMEM((3, owned, half), i16),
            pltpu.VMEM((3, 8, 128), f32),
            pltpu.VMEM((2, n_rows, half + 128), bf16),
            pltpu.VMEM((16, 128), jnp.int32),
            pltpu.VMEM((16, owned, width), bf16),
            pltpu.VMEM((16, owned, width), bf16),
            pltpu.VMEM((n_rows, width), bf16),
            pltpu.VMEM((n_rows, width), bf16),
            pltpu.VMEM((8, n_rows), f32),
            pltpu.VMEM((2, owned, half), f32),
            pltpu.VMEM((owned, half), bf16),
            pltpu.VMEM((n_rows, owned), f32),
            pltpu.VMEM((n_rows, owned), f32),
            pltpu.SemaphoreType.DMA((5,)),
            pltpu.SemaphoreType.DMA((COPIES,)),
            pltpu.SemaphoreType.DMA((COPIES,)),
        ],
        compiler_params=pltpu.CompilerParams(
            collective_id=0, has_side_effects=True, vmem_limit_bytes=53 * 1024 * 1024
        ),
        cost_estimate=pl.CostEstimate(
            flops=6 * n_rows * 16 * owned * width, bytes_accessed=8 * n_rows * width, transcendentals=0
        ),
        name="lloyd_step",
    )(embeddings, centers, assignment.reshape(n_rows // 128, 128))
    return old_min.reshape(n_rows), refined, new_min.reshape(n_rows)


def on_device(embeddings, centers, assignment):
    wide_rows = embeddings.astype(jnp.float32)
    row_norms = jnp.sum(jnp.square(wide_rows), 1)
    starting = jnp.full((embeddings.shape[0],), jnp.inf, jnp.float32)
    portion = lax.all_gather(centers, "shard", axis=0, tiled=True)
    portion_norms = jnp.sum(jnp.square(portion.astype(jnp.float32)), 1)
    products = lax.dot_general(
        embeddings, portion, (((1,), (1,)), ((), ())), preferred_element_type=jnp.float32
    )
    distance = row_norms[:, None] - 2.0 * products + portion_norms[None, :]
    old_min = jnp.minimum(starting, jnp.min(distance, 1))
    n_shard = lax.axis_size("shard")
    owned = centers.shape[0]
    clusters = owned * n_shard
    labels = assignment[:, 0]
    onehot = (labels[:, None] == jnp.arange(clusters, dtype=jnp.int32)[None, :]).astype(
        jnp.bfloat16
    )
    partial_totals = lax.dot_general(
        onehot, embeddings, (((0,), (0,)), ((), ())), preferred_element_type=jnp.float32
    )
    partial_counts = jnp.sum(onehot, 0, dtype=jnp.float32)
    owner_totals, owner_counts = (
        lax.psum_scatter(partial_totals, "shard", scatter_dimension=0, tiled=True),
        lax.psum_scatter(partial_counts, "shard", scatter_dimension=0, tiled=True),
    )
    totals, counts = lax.psum((owner_totals, owner_counts), "grp")
    refined_centers = totals / counts[:, None]
    portion = lax.all_gather(refined_centers, "shard", axis=0, tiled=True)
    portion_norms = jnp.sum(jnp.square(portion), 1)
    products = lax.dot_general(
        wide_rows,
        portion,
        (((1,), (1,)), ((), ())),
        precision=lax.Precision.HIGHEST,
        preferred_element_type=jnp.float32,
    )
    distance = row_norms[:, None] - 2.0 * products + portion_norms[None, :]
    new_min = jnp.minimum(starting, jnp.min(distance, 1))
    return (old_min, refined_centers, new_min)


def solution(mesh):
    placed = (P(("grp", "shard"), None), P("shard", None), P(("grp", "shard"), None))
    here = dict(mesh.shape) == CHIPS
    return jax.shard_map(
        in_one_kernel if here else on_device,
        mesh=mesh,
        in_specs=placed,
        out_specs=(P(("grp", "shard")), P("shard", None), P(("grp", "shard"))),
        check_vma=False,
    )
```

```python
import jax
import jax.numpy as jnp
from jax import lax
from jax.experimental import pallas as pl
from jax.experimental.pallas import tpu as pltpu
from jax.sharding import PartitionSpec as P

MESH = pl.DeviceIdType.MESH
CHIPS = {"grp": 2, "shard": 16}
SLICES = (3, 2, 1, 0)


def dot_nt(left, right):
    return lax.dot_general(
        left, right, (((1,), (1,)), ((), ())), preferred_element_type=jnp.float32
    )


def square_sums(values):
    wide = values.astype(jnp.float32)
    square = wide * wide
    high = square.astype(jnp.bfloat16)
    low = (square - high.astype(jnp.float32)).astype(jnp.bfloat16)
    ones = jnp.ones((16, values.shape[1]), jnp.bfloat16)
    return dot_nt(ones, high) + dot_nt(ones, low)


def column(row):
    return jnp.broadcast_to(row, (128, 128)).T


def pack(block, whole, meta):
    half = whole.shape[1]
    values, count = block[:, 0:half], block[:, half:]
    most = jnp.maximum(jnp.max(jnp.abs(values), 1, keepdims=True), 1e-30)
    whole[...] = jnp.round(values * (32767.0 / most)).astype(jnp.int32).astype(jnp.int16)
    scale = jnp.broadcast_to(most * (1.0 / 32767.0), count.shape)
    lane = lax.broadcasted_iota(jnp.int32, count.shape, 1)
    meta[...] = jnp.where(lane < 4, count, scale).T[0:8]


def unpack(whole, meta):
    half = whole.shape[1]
    count, scale = column(meta[0:1, :]), column(meta[4:5, :])
    values = whole[...].astype(jnp.int32).astype(jnp.float32)
    return jnp.concatenate([values * jnp.concatenate([scale] * (half // 128), 1), count], 1)


def kernel(
    emb, cen, lab, old_out, refined_out, new_out,
    tot, out1, meta1, in1, min1, out2, meta2, in2, min2, out3, meta3, in3, min3,
    rows, labels, old_all, new_all, here, scaled, norms,
    halves, mine, old_acc, new_acc, local_sem, send_sem, recv_sem,
):
    c = lax.axis_index("grp")
    s = lax.axis_index("shard")
    x, y, z = s % 2, (s // 2) % 2, s // 4
    owned, width = cen.shape
    half = width // 2
    n_rows = emb.shape[0]
    x1, y1 = x + (1 - c) * (1 - 2 * x), y + c * (1 - 2 * y)
    x2, y2 = x + c * (1 - 2 * x), y + (1 - c) * (1 - 2 * y)

    def at(zz, yy, xx):
        return zz * 4 + yy * 2 + xx

    def level(j):
        far = (z + 2 * (j // 2)) % 4
        return far + (j % 2) * (1 - 2 * (far % 2))

    sib = (1 - c, s)
    p1 = (c, at(z, y1, x1))
    p2 = (c, at(z, y2, x2))
    above = [None] + [(c, at(level(j), y, x)) for j in (1, 2, 3)]
    cols = pl.ds(pl.multiple_of(c * half, 128), half)
    other_cols = pl.ds(pl.multiple_of((1 - c) * half, 128), half)

    sent = []

    def send(src, dst, device):
        i = len(sent)
        copy = pltpu.make_async_remote_copy(
            src_ref=src, dst_ref=dst, send_sem=send_sem.at[i], recv_sem=recv_sem.at[i],
            device_id=device, device_id_type=MESH,
        )
        copy.start()
        sent.append(copy)
        return copy

    barrier = pltpu.get_barrier_semaphore()
    for peer in (sib, p1, p2, above[1], above[2], above[3]):
        pl.semaphore_signal(barrier, inc=1, device_id=peer, device_id_type=MESH)
    own_lab = pltpu.make_async_copy(lab, labels.at[pl.ds(0, 8)], local_sem.at[3])
    own_lab.start()
    own_emb = pltpu.make_async_copy(emb, here, local_sem.at[4])
    own_emb.start()
    own_rows = pltpu.make_async_copy(emb.at[:, cols], rows.at[0, :, pl.ds(0, half)], local_sem.at[0])
    own_rows.start()
    own_old = pltpu.make_async_copy(cen, old_all.at[s], local_sem.at[1])
    own_old.start()
    rows[:, :, half:] = jnp.ones((2, n_rows, 128), jnp.bfloat16)
    old_acc[...] = jnp.full(old_acc.shape, jnp.inf, jnp.float32)
    new_acc[...] = jnp.full(new_acc.shape, jnp.inf, jnp.float32)
    pl.semaphore_wait(barrier, 6)

    rows_in = send(emb.at[:, other_cols], rows.at[1, :, pl.ds(0, half)], sib)
    labels_in = send(lab, labels.at[pl.ds(8, 8)], sib)

    class Gather:
        def __init__(self, own, buf, share_own):
            self.buf = buf
            spot = buf.at[s, :, cols]
            self.z = [None] + [send(own, spot, above[j]) for j in (1, 2, 3)]
            self.d1 = [send(own, spot, p1)]
            self.d2 = [send(own, spot, p2)]
            self.fz = [send(own, spot, sib) if share_own else None]
            self.f1, self.f2, self.far, self.ffar = [], [], [], []

        def spot(self, j, yy, xx):
            return self.buf.at[at(level(j), yy, xx), :, cols]

        def along_z(self, *which):
            for j in which:
                self.z[j].wait_recv()
                spot = self.spot(j, y, x)
                self.d1.append(send(spot, spot, p1))
                self.d2.append(send(spot, spot, p2))
                self.fz.append(send(spot, spot, sib))

        def along_d1(self, *which):
            for j in which:
                self.d1[j].wait_recv()
                spot = self.spot(j, y1, x1)
                self.far.append(send(spot, spot, p2))
                self.f1.append(send(spot, spot, sib))

        def along_d2(self, *which):
            for j in which:
                self.d2[j].wait_recv()
                spot = self.spot(j, y2, x2)
                self.f2.append(send(spot, spot, sib))

        def last(self, *which):
            for j in which:
                self.far[j].wait_recv()
                spot = self.spot(j, 1 - y, 1 - x)
                self.ffar.append(send(spot, spot, sib))

        def need(self, copies):
            for copy in copies:
                if copy is not None:
                    copy.wait_recv()

    def nearest(buf, acc, yy, xx, start=0, stop=2):
        def pair(i, carry):
            far = (z + 2 * i) % 4
            first = at(far, yy, xx)
            second = at(far + 1 - 2 * (far % 2), yy, xx)
            block = jnp.concatenate([buf[first], buf[second]], 0)
            distance = dot_nt(scaled[...], block) + square_sums(block)[0:1, :]
            near = jnp.minimum(distance[:, :owned], distance[:, owned:])
            acc[...] = jnp.minimum(acc[...], near)
            return carry

        lax.fori_loop(start, stop, pair, 0)

    old = Gather(cen.at[:, cols], old_all, False)

    own_lab.wait()
    own_rows.wait()

    def partial(j, fa, first=False):
        hot = []
        for fb in range(2):
            xa = x + fa * (x1 - x) + fb * (x2 - x)
            ya = y + fa * (y1 - y) + fb * (y2 - y)
            hot.append(lax.broadcasted_iota(jnp.int32, (owned, 128), 0) + at(level(j), ya, xa) * owned)
        ids = jnp.concatenate(hot, 0)

        def one(g, part):
            hot = [
                (labels[pl.ds(8 * g + r, 1), :] == ids).astype(jnp.float32).astype(jnp.bfloat16)
                for r in range(8)
            ]
            block = jnp.concatenate(hot, 1)
            return part + jnp.dot(block, rows[g], preferred_element_type=jnp.float32)

        part = one(0, jnp.zeros((2 * owned, half + 128), jnp.float32))
        if first:
            rows_in.wait_recv()
            labels_in.wait_recv()
        return one(1, part)

    stage1, stage2, stage3 = {}, {}, {}

    def begin(j):
        part = partial(j, 1, j == SLICES[0])
        for fb in range(2):
            pack(part[fb * owned : (fb + 1) * owned], out1.at[j, fb], meta1.at[j, fb])
        stage1[j] = (send(out1.at[j], in1.at[j], p1), send(meta1.at[j], min1.at[j], p1))
        part = partial(j, 0)
        for fb in range(2):
            tot[2 * j + fb] = part[fb * owned : (fb + 1) * owned]

    def middle(j):
        for copy in stage1[j]:
            copy.wait_recv()
        pack(tot[2 * j + 1] + unpack(in1.at[j, 1], min1.at[j, 1]), out2.at[j], meta2.at[j])
        stage2[j] = (send(out2.at[j], in2.at[j], p2), send(meta2.at[j], min2.at[j], p2))
        tot[2 * j] += unpack(in1.at[j, 0], min1.at[j, 0])

    def settle(j):
        for copy in stage2[j]:
            copy.wait_recv()
        tot[2 * j] += unpack(in2.at[j], min2.at[j])
        if j > 0:
            i = j - 1
            pack(tot[2 * j], out3.at[i], meta3.at[i])
            stage3[j] = (send(out3.at[i], in3.at[i], above[j]), send(meta3.at[i], min3.at[i], above[j]))

    begin(SLICES[0])
    begin(SLICES[1])
    middle(SLICES[0])
    own_emb.wait()
    wide = here[...]
    scaled[...] = wide * jnp.asarray(-2.0, jnp.bfloat16)
    norms[...] = square_sums(wide)[0:8, :]

    begin(SLICES[2])
    middle(SLICES[1])
    old.along_z(1, 2, 3)
    settle(SLICES[0])
    begin(SLICES[3])
    middle(SLICES[2])
    settle(SLICES[1])
    old.along_d1(0, 1, 2, 3)
    middle(SLICES[3])
    settle(SLICES[2])
    own_old.wait()
    old.need(old.fz)
    nearest(old_all, old_acc, y, x)
    settle(SLICES[3])
    old.along_d2(0, 1, 2, 3)

    total = tot[0]
    for j in SLICES[:3]:
        for copy in stage3[j]:
            copy.wait_recv()
        total += unpack(in3.at[j - 1], min3.at[j - 1])
    refined = total[:, 0:half] / jnp.concatenate([total[:, half:]] * (half // 128), 1)
    halves[c] = refined
    mine[...] = refined.astype(jnp.bfloat16)
    own_new = pltpu.make_async_copy(mine, new_all.at[s, :, cols], local_sem.at[2])
    own_new.start()
    new = Gather(mine, new_all, True)
    half_in = send(halves.at[c], halves.at[c], sib)

    new.along_z(1)
    new.along_z(2)
    old.need(old.f1 + old.f2)
    nearest(old_all, old_acc, y1, x1)
    new.along_z(3)
    new.along_d1(0, 1)
    old.last(0, 1, 2, 3)
    nearest(old_all, old_acc, y2, x2)
    new.along_d1(2, 3)
    new.along_d2(0, 1, 2, 3)
    old.need(old.ffar)
    nearest(old_all, old_acc, 1 - y, 1 - x)
    new.last(0, 1)
    old_out[...] = jnp.min(old_acc[...].T, 0, keepdims=True) + norms[0:1, :]
    half_in.wait_recv()
    refined_out[:, 0:half] = halves[0]
    refined_out[:, half:width] = halves[1]
    own_new.wait()
    new.need(new.fz)
    nearest(new_all, new_acc, y, x)
    new.last(2, 3)
    new.need(new.f1 + new.f2)
    nearest(new_all, new_acc, y1, x1)
    nearest(new_all, new_acc, y2, x2)
    new.need(new.ffar[:2])
    nearest(new_all, new_acc, 1 - y, 1 - x, 0, 1)
    new.need(new.ffar[2:])
    nearest(new_all, new_acc, 1 - y, 1 - x, 1, 2)
    new_out[...] = jnp.min(new_acc[...].T, 0, keepdims=True) + norms[0:1, :]
    for copy in sent:
        copy.wait_send()


COPIES = 96


def in_one_kernel(embeddings, centers, assignment):
    n_rows, width = embeddings.shape
    owned = centers.shape[0]
    half = width // 2
    f32, bf16, i16 = jnp.float32, jnp.bfloat16, jnp.int16
    vmem = pl.BlockSpec(memory_space=pltpu.VMEM)
    old_min, refined, new_min = pl.pallas_call(
        kernel,
        out_shape=(
            jax.ShapeDtypeStruct((1, n_rows), f32),
            jax.ShapeDtypeStruct((owned, width), f32),
            jax.ShapeDtypeStruct((1, n_rows), f32),
        ),
        in_specs=[pl.BlockSpec(memory_space=pl.ANY)] * 3,
        out_specs=(vmem,) * 3,
        scratch_shapes=[
            pltpu.VMEM((8, owned, half + 128), f32),
            pltpu.VMEM((4, 2, owned, half), i16),
            pltpu.VMEM((4, 2, 8, 128), f32),
            pltpu.VMEM((4, 2, owned, half), i16),
            pltpu.VMEM((4, 2, 8, 128), f32),
            pltpu.VMEM((4, owned, half), i16),
            pltpu.VMEM((4, 8, 128), f32),
            pltpu.VMEM((4, owned, half), i16),
            pltpu.VMEM((4, 8, 128), f32),
            pltpu.VMEM((3, owned, half), i16),
            pltpu.VMEM((3, 8, 128), f32),
            pltpu.VMEM((3, owned, half), i16),
            pltpu.VMEM((3, 8, 128), f32),
            pltpu.VMEM((2, n_rows, half + 128), bf16),
            pltpu.VMEM((16, 128), jnp.int32),
            pltpu.VMEM((16, owned, width), bf16),
            pltpu.VMEM((16, owned, width), bf16),
            pltpu.VMEM((n_rows, width), bf16),
            pltpu.VMEM((n_rows, width), bf16),
            pltpu.VMEM((8, n_rows), f32),
            pltpu.VMEM((2, owned, half), f32),
            pltpu.VMEM((owned, half), bf16),
            pltpu.VMEM((n_rows, owned), f32),
            pltpu.VMEM((n_rows, owned), f32),
            pltpu.SemaphoreType.DMA((5,)),
            pltpu.SemaphoreType.DMA((COPIES,)),
            pltpu.SemaphoreType.DMA((COPIES,)),
        ],
        compiler_params=pltpu.CompilerParams(
            collective_id=0, has_side_effects=True, vmem_limit_bytes=53 * 1024 * 1024
        ),
        cost_estimate=pl.CostEstimate(
            flops=6 * n_rows * 16 * owned * width, bytes_accessed=8 * n_rows * width, transcendentals=0
        ),
        name="lloyd_step",
    )(embeddings, centers, assignment.reshape(n_rows // 128, 128))
    return old_min.reshape(n_rows), refined, new_min.reshape(n_rows)


def on_device(embeddings, centers, assignment):
    wide_rows = embeddings.astype(jnp.float32)
    row_norms = jnp.sum(jnp.square(wide_rows), 1)
    starting = jnp.full((embeddings.shape[0],), jnp.inf, jnp.float32)
    portion = lax.all_gather(centers, "shard", axis=0, tiled=True)
    portion_norms = jnp.sum(jnp.square(portion.astype(jnp.float32)), 1)
    products = lax.dot_general(
        embeddings, portion, (((1,), (1,)), ((), ())), preferred_element_type=jnp.float32
    )
    distance = row_norms[:, None] - 2.0 * products + portion_norms[None, :]
    old_min = jnp.minimum(starting, jnp.min(distance, 1))
    n_shard = lax.axis_size("shard")
    owned = centers.shape[0]
    clusters = owned * n_shard
    labels = assignment[:, 0]
    onehot = (labels[:, None] == jnp.arange(clusters, dtype=jnp.int32)[None, :]).astype(
        jnp.bfloat16
    )
    partial_totals = lax.dot_general(
        onehot, embeddings, (((0,), (0,)), ((), ())), preferred_element_type=jnp.float32
    )
    partial_counts = jnp.sum(onehot, 0, dtype=jnp.float32)
    owner_totals, owner_counts = (
        lax.psum_scatter(partial_totals, "shard", scatter_dimension=0, tiled=True),
        lax.psum_scatter(partial_counts, "shard", scatter_dimension=0, tiled=True),
    )
    totals, counts = lax.psum((owner_totals, owner_counts), "grp")
    refined_centers = totals / counts[:, None]
    portion = lax.all_gather(refined_centers, "shard", axis=0, tiled=True)
    portion_norms = jnp.sum(jnp.square(portion), 1)
    products = lax.dot_general(
        wide_rows,
        portion,
        (((1,), (1,)), ((), ())),
        precision=lax.Precision.HIGHEST,
        preferred_element_type=jnp.float32,
    )
    distance = row_norms[:, None] - 2.0 * products + portion_norms[None, :]
    new_min = jnp.minimum(starting, jnp.min(distance, 1))
    return (old_min, refined_centers, new_min)


def solution(mesh):
    placed = (P(("grp", "shard"), None), P("shard", None), P(("grp", "shard"), None))
    here = dict(mesh.shape) == CHIPS
    return jax.shard_map(
        in_one_kernel if here else on_device,
        mesh=mesh,
        in_specs=placed,
        out_specs=(P(("grp", "shard")), P("shard", None), P(("grp", "shard"))),
        check_vma=False,
    )
```
